512 devices in a mesh: orb: 32 (over y, x), aux: 16 (over z, core).
Axes of the slice: x: 4, y: 8, z: 8, core: 2. Of those that a mesh axis runs over, the one named last changes fastest.
Arguments:
- three_center: bfloat16 [4096, 18432], P('orb', 'aux'), may hold values from -6 to 6
- metric_tensor: bfloat16 [4096, 18432], P('orb', 'aux'), may hold values from -0.046875 to 0.046875
- density: bfloat16 [4096, 144], P('orb'), may hold values from -0.5 to 0.5
- pattern: int32 [256, 9], P('orb'), may hold values 0 or 1
- block_size: int32 [256], replicated, may hold values from 8 to 16
Outputs:
- exchange: bfloat16 [4096, 144], P(('orb', 'aux'))
The draws below stay inside these ranges and needn't reach their ends.
All inputs are finite; a program needn't handle non-finite values. No bound on the sum of `pattern` on one device may be relied on, other than what follows from the above.
Results may differ from the reference program's by a relative error of at most 0.0049.
Values may be sent and summed in bfloat16 or wider, within the bound.
No kernel may reach another device: no remote copies, remote signals or barrier semaphores. Data moves between devices by JAX's collectives and lax.ppermute only.
A program may use at most 64 MiB of HBM per device.

```python
import jax
import jax.numpy as jnp
from jax import lax

PB = 128
BS = 16
H = 4
NBAND = 9
NAT = 256


def with_ends(drawn, key, smallest, largest):
    extent = drawn.shape
    index_at = [jax.random.randint(jax.random.fold_in(key, axis), (), 0, extent[axis]) for axis in range(len(extent))]
    drawn = drawn.at[tuple(index_at)].set(smallest)
    longest = extent.index(max(extent))
    index_at[longest] = (index_at[longest] + 1) % extent[longest]
    return drawn.at[tuple(index_at)].set(largest)


def shard_levels(stream_key, dims, cuts, smallest, top_value):
    factor_of = 1.0
    for axis_at, parts in cuts:
        draws = jax.random.uniform(jax.random.fold_in(jax.random.fold_in(stream_key, 6), axis_at), (parts,), jnp.float32, smallest / len(cuts), top_value / len(cuts))
        factor_of = factor_of * jnp.repeat(jnp.exp(draws), dims[axis_at] // parts).reshape((-1,) + (1,) * (len(dims) - 1 - axis_at))
    return factor_of


def centred(own_key, shape, width, bound, cuts=(), held_as=jnp.bfloat16):
    array = jax.random.normal(own_key, shape, jnp.float32) * width
    if len(cuts) > 0:
        array = shard_levels(own_key, shape, cuts, -0.22, 0.18) * array
    return jnp.clip(array, min=-bound, max=bound).astype(held_as)


def setup_inputs(seed: int = 0) -> dict:
    seeds = jax.random.split(jax.random.key(seed), 6)
    three_center = centred(seeds[0], (NAT * BS, PB * NBAND * BS), 1.0, 6.0, ((0, 32), (1, 16)))
    metric_tensor = centred(seeds[1], (NAT * BS, PB * NBAND * BS), (PB * BS * NBAND) ** -0.5, 0.046875, ((0, 32), (1, 16)))
    density = centred(seeds[2], (NAT * BS, NBAND * BS), (BS * NBAND) ** -0.5, 0.5, ((0, 32),))
    pattern = with_ends((jax.random.randint(seeds[3], (NAT, NBAND), 0, 4) < 3).astype(jnp.int32), jax.random.fold_in(seeds[3], 1), 0, 1)
    block_size = with_ends(jax.random.randint(seeds[4], (NAT,), BS // 2, BS + 1), jax.random.fold_in(seeds[4], 1), BS // 2, BS).astype(jnp.int32)
    return dict(three_center=three_center, metric_tensor=metric_tensor, density=density, pattern=pattern, block_size=block_size)


def slot_shift(values, offset, along):
    length = values.shape[along]
    if offset == 0:
        return values
    zero_shape = list(values.shape)
    zero_shape[along] = abs(offset)
    zeros = jnp.zeros(zero_shape, values.dtype)
    if offset > 0:
        return jnp.concatenate([zeros, lax.slice_in_dim(values, 0, length - offset, axis=along)], axis=along)
    return jnp.concatenate([lax.slice_in_dim(values, -offset, length, axis=along), zeros], axis=along)


def keep_mask(pattern, block_size):
    func_ids = jnp.arange(BS, dtype=jnp.int32)
    is_live = func_ids[None, :] < block_size[:, None]
    col_live = jnp.stack([jnp.roll(is_live, -(slot - H), axis=0) for slot in range(NBAND)], axis=1)
    kept = is_live[:, :, None, None] & (pattern[:, None, :, None] > 0) & col_live[:, None, :, :]
    return kept.reshape(NAT * BS, NBAND * BS)


def reference(three_center, metric_tensor, density, pattern, block_size):
    kept = keep_mask(pattern, block_size)
    zero_value = jnp.zeros((), jnp.bfloat16)
    tensor_full = jnp.transpose(three_center.reshape(NAT * BS, PB, NBAND * BS), (1, 0, 2))
    metric_full = jnp.transpose(metric_tensor.reshape(NAT * BS, PB, NBAND * BS), (1, 0, 2))
    tensor_live = jnp.where(kept[None], tensor_full, zero_value)
    metric_live = jnp.where(kept[None], metric_full, zero_value)
    density_live = jnp.where(kept, density, zero_value).reshape(NAT, BS, NBAND, BS)
    pieces = [slot_shift(jnp.roll(density_live, -(slot - H), axis=0), slot - H, 2) for slot in range(NBAND)]
    spread = jnp.stack(pieces, axis=1).reshape(NAT, NBAND * BS, NBAND * BS).astype(jnp.float32)

    def one_function(summed, function_index):
        left_rows = lax.dynamic_index_in_dim(tensor_live, function_index, 0, keepdims=False)
        left_rows = left_rows.reshape(NAT, BS, NBAND * BS).astype(jnp.float32)
        contracted = jnp.einsum('amk,akn->amn', left_rows, spread).astype(jnp.bfloat16)
        contracted = contracted.reshape(NAT, BS, NBAND, BS).astype(jnp.float32)
        partner = lax.dynamic_index_in_dim(metric_live, function_index, 0, keepdims=False)
        partner = partner.reshape(NAT, BS, NBAND, BS)
        slot_terms = []
        for slot in range(NBAND):
            shifted = slot_shift(jnp.roll(partner, -(slot - H), axis=0), slot - H, 2).astype(jnp.float32)
            slot_terms.append(jnp.einsum('amtg,antg->amn', contracted, shifted))
        return summed + jnp.stack(slot_terms, axis=2), None

    summed, _ = lax.scan(one_function, jnp.zeros((NAT, BS, NBAND, BS), jnp.float32), jnp.arange(PB, dtype=jnp.int32))
    summed = summed * pattern.astype(jnp.float32)[:, None, :, None]
    return summed.reshape(NAT * BS, NBAND * BS).astype(jnp.bfloat16)
```

```python
import jax
import jax.numpy as jnp
from jax import lax
from jax.experimental import pallas as pl
from jax.experimental.pallas import tpu as pltpu
from jax.sharding import PartitionSpec as P

BS = 16
HALF = 4
SLOTS = 2 * HALF + 1
WIDTH = SLOTS * BS
ATOMS = 8
ROWS = ATOMS * BS
SIDE = HALF * BS
WINDOW = (ATOMS + 2 * HALF) * BS
LANES = 128
VMEM = pl.BlockSpec(memory_space=pltpu.VMEM)
SMEM = pl.BlockSpec(memory_space=pltpu.SMEM)


def iota(shape, dim):
    return lax.broadcasted_iota(jnp.int32, shape, dim)


def window_sizes(size_ref):
    total = size_ref.shape[0]
    first = lax.axis_index("orb") * ATOMS + total - HALF
    return [size_ref[lax.rem(first + c, total)] for c in range(ATOMS + 2 * HALF)]


def kept_rows(pattern_ref, sizes):
    shape = (ATOMS, 2 * LANES)
    atom, lane = iota(shape, 0), iota(shape, 1)
    slot, func = lane // BS, lane % BS
    pattern = pattern_ref[...]
    live = jnp.zeros(shape, jnp.int32)
    for c, size in enumerate(sizes):
        live = jnp.where(atom + slot == c, size, live)
    on = jnp.zeros(shape, jnp.int32)
    for k in range(SLOTS):
        on = jnp.where(slot == k, pattern[:, k : k + 1], on)
    cols = jnp.where((func < live) & (on > 0), 1.0, 0.0)
    blocks = []
    for a in range(ATOMS):
        row = iota((BS, 2 * LANES), 0)
        block = jnp.broadcast_to(cols[a : a + 1], (BS, 2 * LANES))
        blocks.append(jnp.where(row < sizes[a + HALF], block, 0.0))
    return blocks


def moved(tile, shift):
    shift = shift % tile.shape[1]
    return tile if shift == 0 else pltpu.roll(tile, shift, 1)


def banded(ref, rows, start, shift, count):
    base = start - shift
    low = base // LANES
    off = base - low * LANES
    last = ref.shape[1] // LANES
    need = count + (1 if off else 0)
    tiles = []
    for i in range(low, low + need):
        i = min(max(i, 0), last - 1)
        tiles.append(ref[rows, i * LANES : (i + 1) * LANES])
    if not off:
        return jnp.concatenate(tiles, axis=1) if count > 1 else tiles[0]
    rolled = [pltpu.roll(t, LANES - off, 1) for t in tiles]
    lane = iota((BS, LANES), 1)
    out = [jnp.where(lane < LANES - off, rolled[i], rolled[i + 1]) for i in range(count)]
    return jnp.concatenate(out, axis=1) if count > 1 else out[0]


def pack_kernel(metric_ref, density_ref, pattern_ref, size_ref, up_ref, down_ref):
    sizes = window_sizes(size_ref)
    kept = kept_rows(pattern_ref, sizes)
    funcs = metric_ref.shape[1] // WIDTH
    for a in range(ATOMS):
        rows = slice(a * BS, (a + 1) * BS)
        if a < HALF:
            out_ref, out_rows = down_ref, slice(a * BS, (a + 1) * BS)
            shift = (2 * HALF + ATOMS - HALF + a - HALF) * BS - LANES
        else:
            out_ref, out_rows = up_ref, slice((a - HALF) * BS, (a - HALF + 1) * BS)
            shift = (a - ATOMS) * BS
        lane = iota((BS, 2 * LANES), 1)
        mask = moved(jnp.where(lane < WIDTH, kept[a], 0.0), shift)[:, :LANES]
        col = iota((BS, LANES), 1)
        inside = (col >= shift) & (col < shift + WIDTH)
        mask = jnp.where(inside, mask, 0.0).astype(jnp.bfloat16)
        for p in range(funcs):
            tile = banded(metric_ref, rows, p * WIDTH, shift, 1)
            out_ref[out_rows, p * LANES : (p + 1) * LANES] = tile * mask
        padded = jnp.concatenate(
            [density_ref[rows, :], jnp.zeros((BS, 2 * LANES - WIDTH), jnp.bfloat16)], axis=1
        )
        tile = moved(padded, shift)[:, :LANES]
        out_ref[out_rows, funcs * LANES : (funcs + 1) * LANES] = tile * mask


def main_kernel(
    three_ref,
    metric_ref,
    density_ref,
    pattern_ref,
    size_ref,
    before_ref,
    after_ref,
    out_ref,
    three_win,
    metric_win,
    density_win,
):
    sizes = window_sizes(size_ref)
    kept = kept_rows(pattern_ref, sizes)
    funcs = metric_ref.shape[1] // WIDTH
    lane = iota((BS, 2 * LANES), 1)
    kept = [jnp.where(lane < WIDTH, block, 0.0) for block in kept]
    zero_side = jnp.zeros((SIDE, LANES), jnp.bfloat16)
    density_win[0:SIDE, 0:LANES] = before_ref[:, funcs * LANES : (funcs + 1) * LANES]
    density_win[0:SIDE, LANES:] = zero_side
    density_win[SIDE + ROWS :, 0:LANES] = zero_side
    density_win[SIDE + ROWS :, LANES:] = after_ref[:, funcs * LANES : (funcs + 1) * LANES]
    for a in range(ATOMS):
        rows = slice(a * BS, (a + 1) * BS)
        mask = moved(kept[a], a * BS).astype(jnp.bfloat16)
        padded = jnp.concatenate(
            [density_ref[rows, :], jnp.zeros((BS, 2 * LANES - WIDTH), jnp.bfloat16)], axis=1
        )
        density_win[SIDE + a * BS : SIDE + (a + 1) * BS, :] = moved(padded, a * BS) * mask
        for p in range(funcs):
            three_win[p, rows, :] = banded(three_ref, rows, p * WIDTH, a * BS, 2) * mask
            metric_win[p, rows, :] = banded(metric_ref, rows, p * WIDTH, a * BS, 2) * mask
    atom = iota((ROWS, WINDOW), 0) // BS
    slot = iota((ROWS, WINDOW), 1) // BS - atom
    in_band = (slot >= 0) & (slot < SLOTS)
    density_all = density_win[...]
    contract_cols = (((1,), (1,)), ((), ()))
    own = jnp.zeros((ROWS, ROWS), jnp.float32)
    left = jnp.zeros((ROWS, SIDE), jnp.float32)
    right = jnp.zeros((ROWS, SIDE), jnp.float32)
    for p in range(funcs):
        spread = jnp.dot(three_win[p], density_all, preferred_element_type=jnp.float32)
        contracted = jnp.where(in_band, spread, 0.0).astype(jnp.bfloat16)
        cols = slice(p * LANES, (p + 1) * LANES)
        own += lax.dot_general(
            contracted, metric_win[p], contract_cols, preferred_element_type=jnp.float32
        )
        left += lax.dot_general(
            contracted[:, :LANES],
            before_ref[:, cols],
            contract_cols,
            preferred_element_type=jnp.float32,
        )
        right += lax.dot_general(
            contracted[:, LANES:],
            after_ref[:, cols],
            contract_cols,
            preferred_element_type=jnp.float32,
        )
    total = jnp.concatenate([left, own, right], axis=1)
    for a in range(ATOMS):
        rows = slice(a * BS, (a + 1) * BS)
        block = moved(total[rows], -a * BS) * kept[a]
        for h in range(2):
            out_ref[2 * a + h] = block[h * 8 : (h + 1) * 8, :WIDTH]


def on_device(three_center, metric_tensor, density, pattern, block_size):
    funcs = three_center.shape[1] // WIDTH
    message = jax.ShapeDtypeStruct((SIDE, (funcs + 1) * LANES), jnp.bfloat16)
    up, down = pl.pallas_call(
        pack_kernel,
        out_shape=(message, message),
        in_specs=[VMEM, VMEM, VMEM, SMEM],
        out_specs=(VMEM, VMEM),
        name="pack_halo",
    )(metric_tensor, density, pattern, block_size)
    peers = lax.axis_size("orb")
    onward = [(i, (i + 1) % peers) for i in range(peers)]
    back = [(j, i) for i, j in onward]
    before = lax.ppermute(up, "orb", onward)
    after = lax.ppermute(down, "orb", back)
    partial_sum = pl.pallas_call(
        main_kernel,
        out_shape=jax.ShapeDtypeStruct((ROWS // 8, 8, WIDTH), jnp.float32),
        in_specs=[VMEM, VMEM, VMEM, VMEM, SMEM, VMEM, VMEM],
        out_specs=VMEM,
        scratch_shapes=[
            pltpu.VMEM((funcs, ROWS, WINDOW), jnp.bfloat16),
            pltpu.VMEM((funcs, ROWS, WINDOW), jnp.bfloat16),
            pltpu.VMEM((WINDOW, WINDOW), jnp.bfloat16),
        ],
        name="exchange_terms",
    )(three_center, metric_tensor, density, pattern, block_size, before, after)
    terms = lax.all_to_all(partial_sum, "aux", 0, 0)
    return jnp.sum(terms, axis=0).astype(jnp.bfloat16)


def solution(mesh):
    placed = (P("orb", "aux"), P("orb", "aux"), P("orb", None), P("orb", None), P())
    return jax.shard_map(
        on_device, mesh=mesh, in_specs=placed, out_specs=P(("orb", "aux"), None), check_vma=False
    )
```

```python
import jax
import jax.numpy as jnp
from jax import lax
from jax.experimental import pallas as pl
from jax.experimental.pallas import tpu as pltpu
from jax.sharding import PartitionSpec as P

BS = 16
HALF = 4
SLOTS = 2 * HALF + 1
WIDTH = SLOTS * BS
ATOMS = 8
ROWS = ATOMS * BS
SIDE = HALF * BS
WINDOW = (ATOMS + 2 * HALF) * BS
LANES = 128
PER = LANES // BS
VMEM = pl.BlockSpec(memory_space=pltpu.VMEM)
SMEM = pl.BlockSpec(memory_space=pltpu.SMEM)
HBM = pl.BlockSpec(memory_space=pltpu.HBM)
GRANT = 8 * 1024 * 1024
NT = (((1,), (1,)), ((), ()))


def iota(shape, dim):
    return lax.broadcasted_iota(jnp.int32, shape, dim)


def window_sizes(size_ref):
    total = size_ref.shape[0]
    first = lax.axis_index("orb") * ATOMS + total - HALF
    return [size_ref[lax.rem(first + c, total)] for c in range(ATOMS + 2 * HALF)]


def by_group(values):
    group = iota((8, LANES), 1) // BS
    out = jnp.zeros((8, LANES), jnp.int32)
    for g, value in values.items():
        out = jnp.where(group == g, value, out)
    return out


def row_mask(pattern_ref, sizes, a, first):
    limit = by_group(
        {
            c - first: pattern_ref[a, c - a] * sizes[c]
            for c in range(first, first + PER)
            if 0 <= c - a < SLOTS
        }
    )
    func = iota((8, LANES), 1) % BS
    row = iota((8, LANES), 0)
    size = sizes[a + HALF]
    halves = [jnp.where((func < limit) & (row + 8 * h < size), 1.0, 0.0) for h in range(2)]
    return jnp.concatenate(halves, axis=0).astype(jnp.bfloat16)


def banded(ref, rows, start, shift, count):
    base = start - shift
    low = base // LANES
    off = base - low * LANES
    last = ref.shape[1] // LANES
    need = count + (1 if off else 0)
    tiles = []
    for i in range(low, low + need):
        i = min(max(i, 0), last - 1)
        tiles.append(ref[rows, i * LANES : (i + 1) * LANES])
    if off:
        rolled = [pltpu.roll(t, LANES - off, 1) for t in tiles]
        lane = iota((BS, LANES), 1)
        tiles = [jnp.where(lane < LANES - off, rolled[i], rolled[i + 1]) for i in range(count)]
    return tiles


def density_rows(spread_ref, pattern_ref, sizes, slot_of, c):
    group = iota((BS, LANES), 1) // BS
    tile = jnp.zeros((BS, LANES), jnp.bfloat16)
    limits = {}
    for j, k in slot_of.items():
        tile = jnp.where(group == j, spread_ref[k * BS : (k + 1) * BS, :], tile)
        limits[j] = pattern_ref[j, k] * sizes[c[j]]
    limit = by_group(limits)
    own = by_group({j: sizes[j + HALF] for j in slot_of})
    live = iota((8, LANES), 1) % BS < own
    row = iota((8, LANES), 0)
    halves = [jnp.where((row + 8 * h < limit) & live, 1.0, 0.0) for h in range(2)]
    return tile * jnp.concatenate(halves, axis=0).astype(jnp.bfloat16)


def pack_halo(metric_ref, spread_ref, pattern_ref, sizes, up_ref, down_ref):
    funcs = metric_ref.shape[1] // WIDTH
    last = slice(funcs * LANES, (funcs + 1) * LANES)
    for a in range(ATOMS):
        rows = slice(a * BS, (a + 1) * BS)
        first = 0 if a < HALF else ATOMS
        out_ref = down_ref if a < HALF else up_ref
        out_rows = slice((a % HALF) * BS, (a % HALF + 1) * BS)
        mask = row_mask(pattern_ref, sizes, a, first)
        for p in range(funcs):
            tile = banded(metric_ref, rows, p * WIDTH, (a - first) * BS, 1)[0]
            out_ref[out_rows, p * LANES : (p + 1) * LANES] = tile * mask
    lane = iota((BS, LANES), 1)
    for g in range(HALF):
        tiles = []
        for c in (g, g + HALF):
            slot_of, atom_of = {}, {}
            for j in range(ATOMS):
                at = c if j < HALF else c + ATOMS
                if 0 <= at - j < SLOTS:
                    slot_of[j], atom_of[j] = at - j, at
            tiles.append(density_rows(spread_ref, pattern_ref, sizes, slot_of, atom_of))
        near, far = tiles[0], pltpu.roll(tiles[1], LANES // 2, 1)
        rows = slice(g * BS, (g + 1) * BS)
        down_ref[rows, last] = jnp.where(lane < LANES // 2, near, far)
        up_ref[rows, last] = jnp.where(lane < LANES // 2, far, near)


def pack_kernel(
    metric_hbm,
    spread_hbm,
    pattern_hbm,
    size_hbm,
    odd_up_ref,
    even_up_ref,
    metric_ref,
    spread_ref,
    pattern_ref,
    size_ref,
    sems,
):
    pairs = (
        (size_hbm, size_ref),
        (pattern_hbm, pattern_ref),
        (spread_hbm, spread_ref),
        (metric_hbm, metric_ref),
    )
    copies = [pltpu.make_async_copy(src, dst, sems.at[i]) for i, (src, dst) in enumerate(pairs)]
    for copy in copies:
        copy.start()
    for copy in copies:
        copy.wait()
    sizes = window_sizes(size_ref)
    odd = lax.rem(lax.axis_index("orb"), 2) == 1

    @pl.when(odd)
    def _():
        pack_halo(metric_ref, spread_ref, pattern_ref, sizes, odd_up_ref, even_up_ref)

    @pl.when(jnp.logical_not(odd))
    def _():
        pack_halo(metric_ref, spread_ref, pattern_ref, sizes, even_up_ref, odd_up_ref)


def prepare_kernel(
    three_ref, metric_ref, spread_ref, pattern_ref, size_ref, three_win, metric_win, spread_win, kept_win
):
    sizes = window_sizes(size_ref)
    funcs = metric_ref.shape[1] // WIDTH
    for a in range(ATOMS):
        rows = slice(a * BS, (a + 1) * BS)
        masks = [row_mask(pattern_ref, sizes, a, h * PER) for h in range(2)]
        for h in range(2):
            kept_win[rows, h * LANES : (h + 1) * LANES] = masks[h]
        for p in range(funcs):
            tiles = banded(three_ref, rows, p * WIDTH, a * BS, 2)
            for h in range(2):
                three_win[p, rows, h * LANES : (h + 1) * LANES] = tiles[h] * masks[h]
            tiles = banded(metric_ref, rows, p * WIDTH, a * BS, 2)
            for h in range(2):
                cols = slice(p * WINDOW + h * LANES, p * WINDOW + (h + 1) * LANES)
                metric_win[rows, cols] = tiles[h] * masks[h]
    lane = iota((BS, LANES), 1)
    zero = jnp.zeros((BS, LANES), jnp.bfloat16)
    for c in range(ATOMS + 2 * HALF):
        slot_of = {j: c - j for j in range(ATOMS) if 0 <= c - j < SLOTS}
        tile = density_rows(spread_ref, pattern_ref, sizes, slot_of, {j: c for j in slot_of})
        tile = pltpu.roll(tile, LANES // 2, 1)
        rows = slice(c * BS, (c + 1) * BS)
        spread_win[rows, :LANES] = jnp.where(lane < LANES // 2, zero, tile)
        spread_win[rows, LANES:] = jnp.where(lane < LANES // 2, tile, zero)


def main_kernel(three_win, metric_win, spread_win, kept_win, even_up_ref, odd_up_ref, out_ref, spread_all):
    funcs = three_win.shape[0]
    last = slice(funcs * LANES, (funcs + 1) * LANES)
    low = iota((SIDE, LANES), 1) < LANES // 2
    odd = lax.rem(lax.axis_index("orb"), 2) == 1

    def before(cols):
        return jnp.where(odd, even_up_ref[:, cols], odd_up_ref[:, cols])

    def after(cols):
        return jnp.where(odd, odd_up_ref[:, cols], even_up_ref[:, cols])

    spread_all[...] = spread_win[...]
    for h in range(2):
        tile = before(last)
        tile = pltpu.roll(tile, LANES // 2, 1) if h == 0 else tile
        rows = slice(h * SIDE, (h + 1) * SIDE)
        spread_all[rows, :LANES] = jnp.where(low, tile, spread_win[rows, :LANES])
        tile = after(last)
        tile = pltpu.roll(tile, LANES // 2, 1) if h == 0 else tile
        rows = slice((h + 2) * SIDE, (h + 3) * SIDE)
        spread_all[rows, LANES:] = jnp.where(low, spread_win[rows, LANES:], tile)
    atom = iota((ROWS, WINDOW), 0) // BS
    slot = iota((ROWS, WINDOW), 1) // BS - atom
    in_band = (slot >= 0) & (slot < SLOTS)
    spread = lax.dot_general(
        three_win[...].reshape(funcs * ROWS, WINDOW), spread_all[...], NT, preferred_element_type=jnp.float32
    )
    contracted = [
        jnp.where(in_band, spread[p * ROWS : (p + 1) * ROWS], 0.0).astype(jnp.bfloat16) for p in range(funcs)
    ]
    own = lax.dot_general(
        jnp.concatenate(contracted, axis=1), metric_win[...], NT, preferred_element_type=jnp.float32
    )
    near = [jnp.concatenate([c[:SIDE, :LANES], c[SIDE:, LANES:]], axis=0) for c in contracted]
    cols = slice(0, funcs * LANES)
    sides = lax.dot_general(
        jnp.concatenate(near, axis=1),
        jnp.concatenate([before(cols), after(cols)], axis=0),
        NT,
        preferred_element_type=jnp.float32,
    )
    total = jnp.concatenate([sides[:, :SIDE], own, sides[:, SIDE:]], axis=1)
    total = jnp.where(kept_win[...] > 0, total, 0.0)
    for a in range(ATOMS):
        block = total[a * BS : (a + 1) * BS]
        block = pltpu.roll(block, WINDOW - a * BS, 1) if a else block
        for h in range(2):
            out_ref[2 * a + h] = block[h * 8 : (h + 1) * 8, :WIDTH]


def call(kernel, out_shape, in_specs, name, flops=0, moved=0, scratch_shapes=()):
    return pl.pallas_call(
        kernel,
        out_shape=out_shape,
        in_specs=in_specs,
        out_specs=(VMEM,) * len(out_shape) if isinstance(out_shape, tuple) else VMEM,
        scratch_shapes=scratch_shapes,
        compiler_params=pltpu.CompilerParams(vmem_limit_bytes=GRANT),
        cost_estimate=pl.CostEstimate(flops=flops, bytes_accessed=moved, transcendentals=0),
        name=name,
    )


def on_device(three_center, metric_tensor, density, pattern, block_size):
    funcs = three_center.shape[1] // WIDTH
    spread = density.T
    message = pltpu.VMEM((SIDE, (funcs + 1) * LANES), jnp.bfloat16)
    odd_up, even_up = call(
        pack_kernel,
        (message, message),
        [HBM] * 4,
        "pack_halo",
        0,
        1 << 20,
        [
            pltpu.VMEM(metric_tensor.shape, jnp.bfloat16),
            pltpu.VMEM(spread.shape, jnp.bfloat16),
            pltpu.SMEM(pattern.shape, jnp.int32),
            pltpu.SMEM(block_size.shape, jnp.int32),
            pltpu.SemaphoreType.DMA((4,)),
        ],
    )(*[pltpu.with_memory_space_constraint(x, pltpu.HBM) for x in (metric_tensor, spread, pattern, block_size)])
    peers = lax.axis_size("orb")
    odd_pairs = [(i, (i + 1) % peers if i % 2 else (i - 1) % peers) for i in range(peers)]
    even_pairs = [(i, i + 1 if i % 2 == 0 else i - 1) for i in range(peers)]
    from_odd_up = lax.ppermute(odd_up, "orb", odd_pairs)
    from_even_up = lax.ppermute(even_up, "orb", even_pairs)
    wide = jax.ShapeDtypeStruct((funcs, ROWS, WINDOW), jnp.bfloat16)
    prepared = call(
        prepare_kernel,
        (
            wide,
            jax.ShapeDtypeStruct((ROWS, funcs * WINDOW), jnp.bfloat16),
            jax.ShapeDtypeStruct((WINDOW, WINDOW), jnp.bfloat16),
            jax.ShapeDtypeStruct((ROWS, WINDOW), jnp.bfloat16),
        ),
        [VMEM, VMEM, VMEM, SMEM, SMEM],
        "window_layout",
        0,
        2 << 20,
    )(three_center, metric_tensor, spread, pattern, block_size)
    partial_sum = call(
        main_kernel,
        jax.ShapeDtypeStruct((ROWS // 8, 8, WIDTH), jnp.float32),
        [VMEM] * 6,
        "exchange_terms",
        1 << 28,
        2 << 20,
        [pltpu.VMEM((WINDOW, WINDOW), jnp.bfloat16)],
    )(*prepared, from_even_up, from_odd_up)
    terms = lax.all_to_all(partial_sum, "aux", 0, 0)
    return jnp.sum(terms, axis=0).astype(jnp.bfloat16)


def solution(mesh):
    placed = (P("orb", "aux"), P("orb", "aux"), P("orb", None), P("orb", None), P())
    return jax.shard_map(
        on_device, mesh=mesh, in_specs=placed, out_specs=P(("orb", "aux"), None), check_vma=False
    )
```

```python
import jax
import jax.numpy as jnp
from jax import lax
from jax.experimental import pallas as pl
from jax.experimental.pallas import tpu as pltpu
from jax.sharding import PartitionSpec as P

BS = 16
HALF = 4
SLOTS = 2 * HALF + 1
WIDTH = SLOTS * BS
ATOMS = 8
ROWS = ATOMS * BS
SIDE = HALF * BS
WINDOW = (ATOMS + 2 * HALF) * BS
LANES = 128
PER = LANES // BS
VMEM = pl.BlockSpec(memory_space=pltpu.VMEM)
SMEM = pl.BlockSpec(memory_space=pltpu.SMEM)
HBM = pl.BlockSpec(memory_space=pltpu.HBM)
GRANT = 8 * 1024 * 1024
NT = (((1,), (1,)), ((), ()))


def iota(shape, dim):
    return lax.broadcasted_iota(jnp.int32, shape, dim)


def window_sizes(size_ref):
    total = size_ref.shape[0]
    first = lax.axis_index("orb") * ATOMS + total - HALF
    return [size_ref[lax.rem(first + c, total)] for c in range(ATOMS + 2 * HALF)]


def by_group(values):
    group = iota((8, LANES), 1) // BS
    out = jnp.zeros((8, LANES), jnp.int32)
    for g, value in values.items():
        out = jnp.where(group == g, value, out)
    return out


def row_mask(pattern_ref, sizes, a, first):
    limit = by_group(
        {
            c - first: pattern_ref[a, c - a] * sizes[c]
            for c in range(first, first + PER)
            if 0 <= c - a < SLOTS
        }
    )
    func = iota((8, LANES), 1) % BS
    row = iota((8, LANES), 0)
    size = sizes[a + HALF]
    halves = [jnp.where((func < limit) & (row + 8 * h < size), 1.0, 0.0) for h in range(2)]
    return jnp.concatenate(halves, axis=0).astype(jnp.bfloat16)


def banded(ref, rows, start, shift, count):
    base = start - shift
    low = base // LANES
    off = base - low * LANES
    last = ref.shape[1] // LANES
    need = count + (1 if off else 0)
    tiles = []
    for i in range(low, low + need):
        i = min(max(i, 0), last - 1)
        tiles.append(ref[rows, i * LANES : (i + 1) * LANES])
    if off:
        rolled = [pltpu.roll(t, LANES - off, 1) for t in tiles]
        lane = iota((BS, LANES), 1)
        tiles = [jnp.where(lane < LANES - off, rolled[i], rolled[i + 1]) for i in range(count)]
    return tiles


def density_rows(spread_ref, pattern_ref, sizes, slot_of, c):
    group = iota((BS, LANES), 1) // BS
    tile = jnp.zeros((BS, LANES), jnp.bfloat16)
    limits = {}
    for j, k in slot_of.items():
        tile = jnp.where(group == j, spread_ref[k * BS : (k + 1) * BS, :], tile)
        limits[j] = pattern_ref[j, k] * sizes[c[j]]
    limit = by_group(limits)
    own = by_group({j: sizes[j + HALF] for j in slot_of})
    live = iota((8, LANES), 1) % BS < own
    row = iota((8, LANES), 0)
    halves = [jnp.where((row + 8 * h < limit) & live, 1.0, 0.0) for h in range(2)]
    return tile * jnp.concatenate(halves, axis=0).astype(jnp.bfloat16)


def pack_halo(metric_ref, spread_ref, pattern_ref, sizes, up_ref, down_ref):
    funcs = metric_ref.shape[1] // WIDTH
    last = slice(funcs * LANES, (funcs + 1) * LANES)
    for a in range(ATOMS):
        rows = slice(a * BS, (a + 1) * BS)
        first = 0 if a < HALF else ATOMS
        out_ref = down_ref if a < HALF else up_ref
        out_rows = slice((a % HALF) * BS, (a % HALF + 1) * BS)
        mask = row_mask(pattern_ref, sizes, a, first)
        for p in range(funcs):
            tile = banded(metric_ref, rows, p * WIDTH, (a - first) * BS, 1)[0]
            out_ref[out_rows, p * LANES : (p + 1) * LANES] = tile * mask
    lane = iota((BS, LANES), 1)
    for g in range(HALF):
        tiles = []
        for c in (g, g + HALF):
            slot_of, atom_of = {}, {}
            for j in range(ATOMS):
                at = c if j < HALF else c + ATOMS
                if 0 <= at - j < SLOTS:
                    slot_of[j], atom_of[j] = at - j, at
            tiles.append(density_rows(spread_ref, pattern_ref, sizes, slot_of, atom_of))
        near, far = tiles[0], pltpu.roll(tiles[1], LANES // 2, 1)
        rows = slice(g * BS, (g + 1) * BS)
        down_ref[rows, last] = jnp.where(lane < LANES // 2, near, far)
        up_ref[rows, last] = jnp.where(lane < LANES // 2, far, near)


def pack_kernel(
    metric_hbm,
    spread_hbm,
    pattern_hbm,
    size_hbm,
    odd_up_ref,
    even_up_ref,
    metric_ref,
    spread_ref,
    pattern_ref,
    size_ref,
    sems,
):
    pairs = (
        (size_hbm, size_ref),
        (pattern_hbm, pattern_ref),
        (spread_hbm, spread_ref),
        (metric_hbm, metric_ref),
    )
    copies = [pltpu.make_async_copy(src, dst, sems.at[i]) for i, (src, dst) in enumerate(pairs)]
    for copy in copies:
        copy.start()
    for copy in copies:
        copy.wait()
    sizes = window_sizes(size_ref)
    odd = lax.rem(lax.axis_index("orb"), 2) == 1

    @pl.when(odd)
    def _():
        pack_halo(metric_ref, spread_ref, pattern_ref, sizes, odd_up_ref, even_up_ref)

    @pl.when(jnp.logical_not(odd))
    def _():
        pack_halo(metric_ref, spread_ref, pattern_ref, sizes, even_up_ref, odd_up_ref)


def prepare_kernel(
    three_ref, metric_ref, spread_ref, pattern_ref, size_ref, three_win, metric_win, spread_win, kept_win
):
    sizes = window_sizes(size_ref)
    funcs = metric_ref.shape[1] // WIDTH
    for a in range(ATOMS):
        rows = slice(a * BS, (a + 1) * BS)
        masks = [row_mask(pattern_ref, sizes, a, h * PER) for h in range(2)]
        for h in range(2):
            kept_win[rows, h * LANES : (h + 1) * LANES] = masks[h]
        for p in range(funcs):
            tiles = banded(three_ref, rows, p * WIDTH, a * BS, 2)
            for h in range(2):
                three_win[p, rows, h * LANES : (h + 1) * LANES] = tiles[h] * masks[h]
            tiles = banded(metric_ref, rows, p * WIDTH, a * BS, 2)
            for h in range(2):
                cols = slice(p * WINDOW + h * LANES, p * WINDOW + (h + 1) * LANES)
                metric_win[rows, cols] = tiles[h] * masks[h]
    lane = iota((BS, LANES), 1)
    zero = jnp.zeros((BS, LANES), jnp.bfloat16)
    for c in range(ATOMS + 2 * HALF):
        slot_of = {j: c - j for j in range(ATOMS) if 0 <= c - j < SLOTS}
        tile = density_rows(spread_ref, pattern_ref, sizes, slot_of, {j: c for j in slot_of})
        tile = pltpu.roll(tile, LANES // 2, 1)
        rows = slice(c * BS, (c + 1) * BS)
        spread_win[rows, :LANES] = jnp.where(lane < LANES // 2, zero, tile)
        spread_win[rows, LANES:] = jnp.where(lane < LANES // 2, tile, zero)


def main_kernel(three_win, metric_win, spread_win, kept_win, even_up_ref, odd_up_ref, out_ref, spread_all):
    funcs = three_win.shape[0]
    last = slice(funcs * LANES, (funcs + 1) * LANES)
    low = iota((SIDE, LANES), 1) < LANES // 2
    odd = lax.rem(lax.axis_index("orb"), 2) == 1

    def before(cols):
        return jnp.where(odd, even_up_ref[:, cols], odd_up_ref[:, cols])

    def after(cols):
        return jnp.where(odd, odd_up_ref[:, cols], even_up_ref[:, cols])

    spread_all[...] = spread_win[...]
    for h in range(2):
        tile = before(last)
        tile = pltpu.roll(tile, LANES // 2, 1) if h == 0 else tile
        rows = slice(h * SIDE, (h + 1) * SIDE)
        spread_all[rows, :LANES] = jnp.where(low, tile, spread_win[rows, :LANES])
        tile = after(last)
        tile = pltpu.roll(tile, LANES // 2, 1) if h == 0 else tile
        rows = slice((h + 2) * SIDE, (h + 3) * SIDE)
        spread_all[rows, LANES:] = jnp.where(low, spread_win[rows, LANES:], tile)
    atom = iota((ROWS, WINDOW), 0) // BS
    slot = iota((ROWS, WINDOW), 1) // BS - atom
    in_band = (slot >= 0) & (slot < SLOTS)
    spread = lax.dot_general(
        three_win[...].reshape(funcs * ROWS, WINDOW), spread_all[...], NT, preferred_element_type=jnp.float32
    )
    contracted = [
        jnp.where(in_band, spread[p * ROWS : (p + 1) * ROWS], 0.0).astype(jnp.bfloat16) for p in range(funcs)
    ]
    own = lax.dot_general(
        jnp.concatenate(contracted, axis=1), metric_win[...], NT, preferred_element_type=jnp.float32
    )
    near = [jnp.concatenate([c[:SIDE, :LANES], c[SIDE:, LANES:]], axis=0) for c in contracted]
    cols = slice(0, funcs * LANES)
    sides = lax.dot_general(
        jnp.concatenate(near, axis=1),
        jnp.concatenate([before(cols), after(cols)], axis=0),
        NT,
        preferred_element_type=jnp.float32,
    )
    total = jnp.concatenate([sides[:, :SIDE], own, sides[:, SIDE:]], axis=1)
    total = jnp.where(kept_win[...] > 0, total, 0.0)
    for a in range(ATOMS):
        block = total[a * BS : (a + 1) * BS]
        block = pltpu.roll(block, WINDOW - a * BS, 1) if a else block
        for h in range(2):
            out_ref[2 * a + h] = block[h * 8 : (h + 1) * 8, :WIDTH].astype(jnp.bfloat16)


def call(kernel, out_shape, in_specs, name, flops=0, moved=0, scratch_shapes=()):
    return pl.pallas_call(
        kernel,
        out_shape=out_shape,
        in_specs=in_specs,
        out_specs=(VMEM,) * len(out_shape) if isinstance(out_shape, tuple) else VMEM,
        scratch_shapes=scratch_shapes,
        compiler_params=pltpu.CompilerParams(vmem_limit_bytes=GRANT),
        cost_estimate=pl.CostEstimate(flops=flops, bytes_accessed=moved, transcendentals=0),
        name=name,
    )


def on_device(three_center, metric_tensor, density, pattern, block_size):
    funcs = three_center.shape[1] // WIDTH
    spread = density.T
    message = pltpu.VMEM((SIDE, (funcs + 1) * LANES), jnp.bfloat16)
    odd_up, even_up = call(
        pack_kernel,
        (message, message),
        [HBM] * 4,
        "pack_halo",
        0,
        1 << 20,
        [
            pltpu.VMEM(metric_tensor.shape, jnp.bfloat16),
            pltpu.VMEM(spread.shape, jnp.bfloat16),
            pltpu.SMEM(pattern.shape, jnp.int32),
            pltpu.SMEM(block_size.shape, jnp.int32),
            pltpu.SemaphoreType.DMA((4,)),
        ],
    )(*[pltpu.with_memory_space_constraint(x, pltpu.HBM) for x in (metric_tensor, spread, pattern, block_size)])
    peers = lax.axis_size("orb")
    odd_pairs = [(i, (i + 1) % peers if i % 2 else (i - 1) % peers) for i in range(peers)]
    even_pairs = [(i, i + 1 if i % 2 == 0 else i - 1) for i in range(peers)]
    from_odd_up = lax.ppermute(odd_up, "orb", odd_pairs)
    from_even_up = lax.ppermute(even_up, "orb", even_pairs)
    wide = jax.ShapeDtypeStruct((funcs, ROWS, WINDOW), jnp.bfloat16)
    prepared = call(
        prepare_kernel,
        (
            wide,
            jax.ShapeDtypeStruct((ROWS, funcs * WINDOW), jnp.bfloat16),
            jax.ShapeDtypeStruct((WINDOW, WINDOW), jnp.bfloat16),
            jax.ShapeDtypeStruct((ROWS, WINDOW), jnp.bfloat16),
        ),
        [VMEM, VMEM, VMEM, SMEM, SMEM],
        "window_layout",
        0,
        2 << 20,
    )(three_center, metric_tensor, spread, pattern, block_size)
    partial_sum = call(
        main_kernel,
        jax.ShapeDtypeStruct((ROWS // 8, 8, WIDTH), jnp.bfloat16),
        [VMEM] * 6,
        "exchange_terms",
        1 << 28,
        2 << 20,
        [pltpu.VMEM((WINDOW, WINDOW), jnp.bfloat16)],
    )(*prepared, from_even_up, from_odd_up)
    terms = lax.all_to_all(partial_sum, "aux", 0, 0)
    return jnp.sum(terms.astype(jnp.float32), axis=0).astype(jnp.bfloat16)


def solution(mesh):
    placed = (P("orb", "aux"), P("orb", "aux"), P("orb", None), P("orb", None), P())
    return jax.shard_map(
        on_device, mesh=mesh, in_specs=placed, out_specs=P(("orb", "aux"), None), check_vma=False
    )
```

```python
import jax
import jax.numpy as jnp
from jax import lax
from jax.experimental import pallas as pl
from jax.experimental.pallas import tpu as pltpu
from jax.sharding import PartitionSpec as P

BS = 16
HALF = 4
SLOTS = 2 * HALF + 1
WIDTH = SLOTS * BS
ATOMS = 8
ROWS = ATOMS * BS
SIDE = HALF * BS
WINDOW = (ATOMS + 2 * HALF) * BS
LANES = 128
PER = LANES // BS
VMEM = pl.BlockSpec(memory_space=pltpu.VMEM)
SMEM = pl.BlockSpec(memory_space=pltpu.SMEM)
HBM = pl.BlockSpec(memory_space=pltpu.HBM)
GRANT = 8 * 1024 * 1024
NT = (((1,), (1,)), ((), ()))


def iota(shape, dim):
    return lax.broadcasted_iota(jnp.int32, shape, dim)


def window_sizes(size_ref):
    total = size_ref.shape[0]
    first = lax.axis_index("orb") * ATOMS + total - HALF
    return [size_ref[lax.rem(first + c, total)] for c in range(ATOMS + 2 * HALF)]


def by_group(values):
    group = iota((8, LANES), 1) // BS
    out = jnp.zeros((8, LANES), jnp.int32)
    for g, value in values.items():
        out = jnp.where(group == g, value, out)
    return out


def row_mask(pattern_ref, sizes, a, first):
    limit = by_group(
        {
            c - first: pattern_ref[a, c - a] * sizes[c]
            for c in range(first, first + PER)
            if 0 <= c - a < SLOTS
        }
    )
    func = iota((8, LANES), 1) % BS
    row = iota((8, LANES), 0)
    size = sizes[a + HALF]
    halves = [jnp.where((func < limit) & (row + 8 * h < size), 1.0, 0.0) for h in range(2)]
    return jnp.concatenate(halves, axis=0).astype(jnp.bfloat16)


def banded(ref, rows, start, shift, count):
    base = start - shift
    low = base // LANES
    off = base - low * LANES
    last = ref.shape[1] // LANES
    need = count + (1 if off else 0)
    tiles = []
    for i in range(low, low + need):
        i = min(max(i, 0), last - 1)
        tiles.append(ref[rows, i * LANES : (i + 1) * LANES])
    if off:
        rolled = [pltpu.roll(t, LANES - off, 1) for t in tiles]
        lane = iota((BS, LANES), 1)
        tiles = [jnp.where(lane < LANES - off, rolled[i], rolled[i + 1]) for i in range(count)]
    return tiles


def density_rows(spread_ref, pattern_ref, sizes, slot_of, c):
    group = iota((BS, LANES), 1) // BS
    tile = jnp.zeros((BS, LANES), jnp.bfloat16)
    limits = {}
    for j, k in slot_of.items():
        tile = jnp.where(group == j, spread_ref[k * BS : (k + 1) * BS, :], tile)
        limits[j] = pattern_ref[j, k] * sizes[c[j]]
    limit = by_group(limits)
    own = by_group({j: sizes[j + HALF] for j in slot_of})
    live = iota((8, LANES), 1) % BS < own
    row = iota((8, LANES), 0)
    halves = [jnp.where((row + 8 * h < limit) & live, 1.0, 0.0) for h in range(2)]
    return tile * jnp.concatenate(halves, axis=0).astype(jnp.bfloat16)


def pack_halo(metric_ref, spread_ref, pattern_ref, sizes, up_ref, down_ref):
    funcs = metric_ref.shape[1] // WIDTH
    last = slice(funcs * LANES, (funcs + 1) * LANES)
    for a in range(ATOMS):
        rows = slice(a * BS, (a + 1) * BS)
        first = 0 if a < HALF else ATOMS
        out_ref = down_ref if a < HALF else up_ref
        out_rows = slice((a % HALF) * BS, (a % HALF + 1) * BS)
        mask = row_mask(pattern_ref, sizes, a, first)
        for p in range(funcs):
            tile = banded(metric_ref, rows, p * WIDTH, (a - first) * BS, 1)[0]
            out_ref[out_rows, p * LANES : (p + 1) * LANES] = tile * mask
    lane = iota((BS, LANES), 1)
    for g in range(HALF):
        tiles = []
        for c in (g, g + HALF):
            slot_of, atom_of = {}, {}
            for j in range(ATOMS):
                at = c if j < HALF else c + ATOMS
                if 0 <= at - j < SLOTS:
                    slot_of[j], atom_of[j] = at - j, at
            tiles.append(density_rows(spread_ref, pattern_ref, sizes, slot_of, atom_of))
        near, far = tiles[0], pltpu.roll(tiles[1], LANES // 2, 1)
        rows = slice(g * BS, (g + 1) * BS)
        down_ref[rows, last] = jnp.where(lane < LANES // 2, near, far)
        up_ref[rows, last] = jnp.where(lane < LANES // 2, far, near)


def pack_kernel(
    metric_hbm,
    spread_hbm,
    pattern_hbm,
    size_hbm,
    odd_up_ref,
    even_up_ref,
    metric_ref,
    spread_ref,
    pattern_ref,
    size_ref,
    sems,
):
    blocks = [pl.ds(a * BS, BS) for a in range(ATOMS)]
    pairs = (
        (size_hbm, size_ref),
        (pattern_hbm, pattern_ref),
        (spread_hbm, spread_ref),
        *((metric_hbm.at[rows], metric_ref.at[rows]) for rows in blocks),
    )
    copies = [pltpu.make_async_copy(src, dst, sems.at[i]) for i, (src, dst) in enumerate(pairs)]
    for copy in copies:
        copy.start()
    for copy in copies:
        copy.wait()
    sizes = window_sizes(size_ref)
    odd = lax.rem(lax.axis_index("orb"), 2) == 1

    @pl.when(odd)
    def _():
        pack_halo(metric_ref, spread_ref, pattern_ref, sizes, odd_up_ref, even_up_ref)

    @pl.when(jnp.logical_not(odd))
    def _():
        pack_halo(metric_ref, spread_ref, pattern_ref, sizes, even_up_ref, odd_up_ref)


def prepare_kernel(
    three_ref,
    metric_ref,
    spread_ref,
    pattern_ref,
    size_ref,
    message_ref,
    three_win,
    metric_win,
    spread_win,
    kept_win,
    first_ref,
):
    first_ref[...] = message_ref[...]
    sizes = window_sizes(size_ref)
    funcs = metric_ref.shape[1] // WIDTH
    for a in range(ATOMS):
        rows = slice(a * BS, (a + 1) * BS)
        masks = [row_mask(pattern_ref, sizes, a, h * PER) for h in range(2)]
        for h in range(2):
            kept_win[rows, h * LANES : (h + 1) * LANES] = masks[h]
        for p in range(funcs):
            tiles = banded(three_ref, rows, p * WIDTH, a * BS, 2)
            for h in range(2):
                three_win[p, rows, h * LANES : (h + 1) * LANES] = tiles[h] * masks[h]
            tiles = banded(metric_ref, rows, p * WIDTH, a * BS, 2)
            for h in range(2):
                cols = slice(p * WINDOW + h * LANES, p * WINDOW + (h + 1) * LANES)
                metric_win[rows, cols] = tiles[h] * masks[h]
    lane = iota((BS, LANES), 1)
    zero = jnp.zeros((BS, LANES), jnp.bfloat16)
    for c in range(ATOMS + 2 * HALF):
        slot_of = {j: c - j for j in range(ATOMS) if 0 <= c - j < SLOTS}
        tile = density_rows(spread_ref, pattern_ref, sizes, slot_of, {j: c for j in slot_of})
        tile = pltpu.roll(tile, LANES // 2, 1)
        rows = slice(c * BS, (c + 1) * BS)
        spread_win[rows, :LANES] = jnp.where(lane < LANES // 2, zero, tile)
        spread_win[rows, LANES:] = jnp.where(lane < LANES // 2, tile, zero)


def main_kernel(three_win, metric_win, spread_win, kept_win, first_ref, odd_up_ref, even_up_ref, out_ref, spread_all):
    funcs = three_win.shape[0]
    last = slice(funcs * LANES, (funcs + 1) * LANES)
    low = iota((SIDE, LANES), 1) < LANES // 2
    odd = lax.rem(lax.axis_index("orb"), 2) == 1

    is_first = lax.axis_index("orb") == 0

    def even(cols):
        return jnp.where(is_first, first_ref[:, cols], even_up_ref[:, cols])

    def before(cols):
        return jnp.where(odd, even(cols), odd_up_ref[:, cols])

    def after(cols):
        return jnp.where(odd, odd_up_ref[:, cols], even(cols))

    spread_all[...] = spread_win[...]
    for h in range(2):
        tile = before(last)
        tile = pltpu.roll(tile, LANES // 2, 1) if h == 0 else tile
        rows = slice(h * SIDE, (h + 1) * SIDE)
        spread_all[rows, :LANES] = jnp.where(low, tile, spread_win[rows, :LANES])
        tile = after(last)
        tile = pltpu.roll(tile, LANES // 2, 1) if h == 0 else tile
        rows = slice((h + 2) * SIDE, (h + 3) * SIDE)
        spread_all[rows, LANES:] = jnp.where(low, spread_win[rows, LANES:], tile)
    atom = iota((ROWS, WINDOW), 0) // BS
    slot = iota((ROWS, WINDOW), 1) // BS - atom
    in_band = (slot >= 0) & (slot < SLOTS)
    spread = lax.dot_general(
        three_win[...].reshape(funcs * ROWS, WINDOW), spread_all[...], NT, preferred_element_type=jnp.float32
    )
    contracted = [
        jnp.where(in_band, spread[p * ROWS : (p + 1) * ROWS], 0.0).astype(jnp.bfloat16) for p in range(funcs)
    ]
    own = lax.dot_general(
        jnp.concatenate(contracted, axis=1), metric_win[...], NT, preferred_element_type=jnp.float32
    )
    near = [jnp.concatenate([c[:SIDE, :LANES], c[SIDE:, LANES:]], axis=0) for c in contracted]
    cols = slice(0, funcs * LANES)
    sides = lax.dot_general(
        jnp.concatenate(near, axis=1),
        jnp.concatenate([before(cols), after(cols)], axis=0),
        NT,
        preferred_element_type=jnp.float32,
    )
    total = jnp.concatenate([sides[:, :SIDE], own, sides[:, SIDE:]], axis=1)
    total = jnp.where(kept_win[...] > 0, total, 0.0)
    for a in range(ATOMS):
        block = total[a * BS : (a + 1) * BS]
        block = pltpu.roll(block, WINDOW - a * BS, 1) if a else block
        for h in range(2):
            out_ref[2 * a + h] = block[h * 8 : (h + 1) * 8, :WIDTH].astype(jnp.bfloat16)


def call(kernel, out_shape, in_specs, name, flops=0, moved=0, scratch_shapes=()):
    return pl.pallas_call(
        kernel,
        out_shape=out_shape,
        in_specs=in_specs,
        out_specs=(VMEM,) * len(out_shape) if isinstance(out_shape, tuple) else VMEM,
        scratch_shapes=scratch_shapes,
        compiler_params=pltpu.CompilerParams(vmem_limit_bytes=GRANT),
        cost_estimate=pl.CostEstimate(flops=flops, bytes_accessed=moved, transcendentals=0),
        name=name,
    )


def on_device(three_center, metric_tensor, density, pattern, block_size):
    funcs = three_center.shape[1] // WIDTH
    spread = density.T
    message = pltpu.VMEM((SIDE, (funcs + 1) * LANES), jnp.bfloat16)
    odd_up, even_up = call(
        pack_kernel,
        (message, message),
        [HBM] * 4,
        "pack_halo",
        0,
        1 << 20,
        [
            pltpu.VMEM(metric_tensor.shape, jnp.bfloat16),
            pltpu.VMEM(spread.shape, jnp.bfloat16),
            pltpu.SMEM(pattern.shape, jnp.int32),
            pltpu.SMEM(block_size.shape, jnp.int32),
            pltpu.SemaphoreType.DMA((3 + ATOMS,)),
        ],
    )(*[pltpu.with_memory_space_constraint(x, pltpu.HBM) for x in (metric_tensor, spread, pattern, block_size)])
    peers = lax.axis_size("orb")
    odd_pairs = [(i, (i + 1) % peers if i % 2 else (i - 1) % peers) for i in range(peers)]
    even_pairs = [(i, i + 1 if i % 2 == 0 else i - 1) for i in range(peers)]
    ahead = (1, 0)
    from_first_even = lax.ppermute(even_up, "orb", [ahead])
    from_odd_up = lax.ppermute(odd_up, "orb", odd_pairs)
    from_even_up = lax.ppermute(even_up, "orb", [pair for pair in even_pairs if pair != ahead])
    wide = jax.ShapeDtypeStruct((funcs, ROWS, WINDOW), jnp.bfloat16)
    prepared = call(
        prepare_kernel,
        (
            wide,
            jax.ShapeDtypeStruct((ROWS, funcs * WINDOW), jnp.bfloat16),
            jax.ShapeDtypeStruct((WINDOW, WINDOW), jnp.bfloat16),
            jax.ShapeDtypeStruct((ROWS, WINDOW), jnp.bfloat16),
            message,
        ),
        [VMEM, VMEM, VMEM, SMEM, SMEM, VMEM],
        "window_layout",
        0,
        2 << 20,
    )(three_center, metric_tensor, spread, pattern, block_size, from_first_even)
    partial_sum = call(
        main_kernel,
        jax.ShapeDtypeStruct((ROWS // 8, 8, WIDTH), jnp.bfloat16),
        [VMEM] * 7,
        "exchange_terms",
        1 << 28,
        2 << 20,
        [pltpu.VMEM((WINDOW, WINDOW), jnp.bfloat16)],
    )(*prepared, from_odd_up, from_even_up)
    terms = lax.all_to_all(partial_sum, "aux", 0, 0)
    return jnp.sum(terms.astype(jnp.float32), axis=0).astype(jnp.bfloat16)


def solution(mesh):
    placed = (P("orb", "aux"), P("orb", "aux"), P("orb", None), P("orb", None), P())
    return jax.shard_map(
        on_device, mesh=mesh, in_specs=placed, out_specs=P(("orb", "aux"), None), check_vma=False
    )
```

```python
import functools

import jax
import jax.numpy as jnp
from jax import lax
from jax.experimental import pallas as pl
from jax.experimental.pallas import tpu as pltpu
from jax.sharding import PartitionSpec as P

BS = 16
HALF = 4
SLOTS = 2 * HALF + 1
WIDTH = SLOTS * BS
ATOMS = 8
ROWS = ATOMS * BS
SIDE = HALF * BS
WINDOW = (ATOMS + 2 * HALF) * BS
LANES = 128
PER = LANES // BS
VMEM = pl.BlockSpec(memory_space=pltpu.VMEM)
SMEM = pl.BlockSpec(memory_space=pltpu.SMEM)
HBM = pl.BlockSpec(memory_space=pltpu.HBM)
GRANT = 8 * 1024 * 1024
NT = (((1,), (1,)), ((), ()))
AHEAD = (0, 20, 24, 28)


def iota(shape, dim):
    return lax.broadcasted_iota(jnp.int32, shape, dim)


def window_sizes(size_ref):
    total = size_ref.shape[0]
    first = lax.axis_index("orb") * ATOMS + total - HALF
    return [size_ref[lax.rem(first + c, total)] for c in range(ATOMS + 2 * HALF)]


def by_group(values):
    group = iota((8, LANES), 1) // BS
    out = jnp.zeros((8, LANES), jnp.int32)
    for g, value in values.items():
        out = jnp.where(group == g, value, out)
    return out


def row_mask(pattern_ref, sizes, a, first):
    limit = by_group(
        {
            c - first: pattern_ref[a, c - a] * sizes[c]
            for c in range(first, first + PER)
            if 0 <= c - a < SLOTS
        }
    )
    func = iota((8, LANES), 1) % BS
    row = iota((8, LANES), 0)
    size = sizes[a + HALF]
    halves = [jnp.where((func < limit) & (row + 8 * h < size), 1.0, 0.0) for h in range(2)]
    return jnp.concatenate(halves, axis=0).astype(jnp.bfloat16)


def banded(ref, rows, start, shift, count):
    base = start - shift
    low = base // LANES
    off = base - low * LANES
    last = ref.shape[1] // LANES
    need = count + (1 if off else 0)
    tiles = []
    for i in range(low, low + need):
        i = min(max(i, 0), last - 1)
        tiles.append(ref[rows, i * LANES : (i + 1) * LANES])
    if off:
        rolled = [pltpu.roll(t, LANES - off, 1) for t in tiles]
        lane = iota((BS, LANES), 1)
        tiles = [jnp.where(lane < LANES - off, rolled[i], rolled[i + 1]) for i in range(count)]
    return tiles


def density_rows(spread_ref, pattern_ref, sizes, slot_of, c):
    group = iota((BS, LANES), 1) // BS
    tile = jnp.zeros((BS, LANES), jnp.bfloat16)
    limits = {}
    for j, k in slot_of.items():
        tile = jnp.where(group == j, spread_ref[k * BS : (k + 1) * BS, :], tile)
        limits[j] = pattern_ref[j, k] * sizes[c[j]]
    limit = by_group(limits)
    own = by_group({j: sizes[j + HALF] for j in slot_of})
    live = iota((8, LANES), 1) % BS < own
    row = iota((8, LANES), 0)
    halves = [jnp.where((row + 8 * h < limit) & live, 1.0, 0.0) for h in range(2)]
    return tile * jnp.concatenate(halves, axis=0).astype(jnp.bfloat16)


def pack_halo(metric_ref, spread_ref, pattern_ref, sizes, up_ref, down_ref):
    funcs = metric_ref.shape[1] // WIDTH
    last = slice(funcs * LANES, (funcs + 1) * LANES)
    for a in range(ATOMS):
        rows = slice(a * BS, (a + 1) * BS)
        first = 0 if a < HALF else ATOMS
        out_ref = down_ref if a < HALF else up_ref
        out_rows = slice((a % HALF) * BS, (a % HALF + 1) * BS)
        mask = row_mask(pattern_ref, sizes, a, first)
        for p in range(funcs):
            tile = banded(metric_ref, rows, p * WIDTH, (a - first) * BS, 1)[0]
            out_ref[out_rows, p * LANES : (p + 1) * LANES] = tile * mask
    lane = iota((BS, LANES), 1)
    for g in range(HALF):
        tiles = []
        for c in (g, g + HALF):
            slot_of, atom_of = {}, {}
            for j in range(ATOMS):
                at = c if j < HALF else c + ATOMS
                if 0 <= at - j < SLOTS:
                    slot_of[j], atom_of[j] = at - j, at
            tiles.append(density_rows(spread_ref, pattern_ref, sizes, slot_of, atom_of))
        near, far = tiles[0], pltpu.roll(tiles[1], LANES // 2, 1)
        rows = slice(g * BS, (g + 1) * BS)
        down_ref[rows, last] = jnp.where(lane < LANES // 2, near, far)
        up_ref[rows, last] = jnp.where(lane < LANES // 2, far, near)


def pack_kernel(
    metric_hbm,
    spread_hbm,
    pattern_hbm,
    size_hbm,
    odd_up_ref,
    even_up_ref,
    metric_ref,
    spread_ref,
    pattern_ref,
    size_ref,
    sems,
):
    blocks = [pl.ds(a * BS, BS) for a in range(ATOMS)]
    pairs = (
        (size_hbm, size_ref),
        (pattern_hbm, pattern_ref),
        (spread_hbm, spread_ref),
        *((metric_hbm.at[rows], metric_ref.at[rows]) for rows in blocks),
    )
    copies = [pltpu.make_async_copy(src, dst, sems.at[i]) for i, (src, dst) in enumerate(pairs)]
    for copy in copies:
        copy.start()
    for copy in copies:
        copy.wait()
    sizes = window_sizes(size_ref)
    odd = lax.rem(lax.axis_index("orb"), 2) == 1

    @pl.when(odd)
    def _():
        pack_halo(metric_ref, spread_ref, pattern_ref, sizes, odd_up_ref, even_up_ref)

    @pl.when(jnp.logical_not(odd))
    def _():
        pack_halo(metric_ref, spread_ref, pattern_ref, sizes, even_up_ref, odd_up_ref)


def prepare_kernel(
    three_ref,
    metric_ref,
    spread_ref,
    pattern_ref,
    size_ref,
    message_ref,
    three_win,
    metric_win,
    spread_win,
    kept_win,
    first_ref,
):
    first_ref[...] = message_ref[...]
    sizes = window_sizes(size_ref)
    funcs = metric_ref.shape[1] // WIDTH
    for a in range(ATOMS):
        rows = slice(a * BS, (a + 1) * BS)
        masks = [row_mask(pattern_ref, sizes, a, h * PER) for h in range(2)]
        for h in range(2):
            kept_win[rows, h * LANES : (h + 1) * LANES] = masks[h]
        for p in range(funcs):
            tiles = banded(three_ref, rows, p * WIDTH, a * BS, 2)
            for h in range(2):
                three_win[p, rows, h * LANES : (h + 1) * LANES] = tiles[h] * masks[h]
            tiles = banded(metric_ref, rows, p * WIDTH, a * BS, 2)
            for h in range(2):
                cols = slice(p * WINDOW + h * LANES, p * WINDOW + (h + 1) * LANES)
                metric_win[rows, cols] = tiles[h] * masks[h]
    lane = iota((BS, LANES), 1)
    zero = jnp.zeros((BS, LANES), jnp.bfloat16)
    for c in range(ATOMS + 2 * HALF):
        slot_of = {j: c - j for j in range(ATOMS) if 0 <= c - j < SLOTS}
        tile = density_rows(spread_ref, pattern_ref, sizes, slot_of, {j: c for j in slot_of})
        tile = pltpu.roll(tile, LANES // 2, 1)
        rows = slice(c * BS, (c + 1) * BS)
        spread_win[rows, :LANES] = jnp.where(lane < LANES // 2, zero, tile)
        spread_win[rows, LANES:] = jnp.where(lane < LANES // 2, tile, zero)


def main_kernel(place, three_win, metric_win, spread_win, kept_win, first_ref, odd_up_ref, even_up_ref, out_ref, spread_all):
    funcs = three_win.shape[0]
    last = slice(funcs * LANES, (funcs + 1) * LANES)
    low = iota((SIDE, LANES), 1) < LANES // 2
    odd = lax.rem(lax.axis_index("orb"), 2) == 1

    here = lax.axis_index("orb")
    is_first = lax.rem(lax.axis_index("aux"), 2) == 1
    for target in AHEAD:
        is_first |= here == target

    def even(cols):
        return jnp.where(is_first, first_ref[:, cols], even_up_ref[:, cols])

    def before(cols):
        return jnp.where(odd, even(cols), odd_up_ref[:, cols])

    def after(cols):
        return jnp.where(odd, odd_up_ref[:, cols], even(cols))

    spread_all[...] = spread_win[...]
    for h in range(2):
        tile = before(last)
        tile = pltpu.roll(tile, LANES // 2, 1) if h == 0 else tile
        rows = slice(h * SIDE, (h + 1) * SIDE)
        spread_all[rows, :LANES] = jnp.where(low, tile, spread_win[rows, :LANES])
        tile = after(last)
        tile = pltpu.roll(tile, LANES // 2, 1) if h == 0 else tile
        rows = slice((h + 2) * SIDE, (h + 3) * SIDE)
        spread_all[rows, LANES:] = jnp.where(low, spread_win[rows, LANES:], tile)
    atom = iota((ROWS, WINDOW), 0) // BS
    slot = iota((ROWS, WINDOW), 1) // BS - atom
    in_band = (slot >= 0) & (slot < SLOTS)
    spread = lax.dot_general(
        three_win[...].reshape(funcs * ROWS, WINDOW), spread_all[...], NT, preferred_element_type=jnp.float32
    )
    contracted = [
        jnp.where(in_band, spread[p * ROWS : (p + 1) * ROWS], 0.0).astype(jnp.bfloat16) for p in range(funcs)
    ]
    own = lax.dot_general(
        jnp.concatenate(contracted, axis=1), metric_win[...], NT, preferred_element_type=jnp.float32
    )
    near = [jnp.concatenate([c[:SIDE, :LANES], c[SIDE:, LANES:]], axis=0) for c in contracted]
    cols = slice(0, funcs * LANES)
    sides = lax.dot_general(
        jnp.concatenate(near, axis=1),
        jnp.concatenate([before(cols), after(cols)], axis=0),
        NT,
        preferred_element_type=jnp.float32,
    )
    total = jnp.concatenate([sides[:, :SIDE], own, sides[:, SIDE:]], axis=1)
    total = jnp.where(kept_win[...] > 0, total, 0.0)
    for a in range(ATOMS):
        block = total[a * BS : (a + 1) * BS]
        block = pltpu.roll(block, WINDOW - a * BS, 1) if a else block
        for h in range(2):
            out_ref[place[2 * a + h]] = block[h * 8 : (h + 1) * 8, :WIDTH].astype(jnp.bfloat16)


def call(kernel, out_shape, in_specs, name, flops=0, moved=0, scratch_shapes=()):
    return pl.pallas_call(
        kernel,
        out_shape=out_shape,
        in_specs=in_specs,
        out_specs=(VMEM,) * len(out_shape) if isinstance(out_shape, tuple) else VMEM,
        scratch_shapes=scratch_shapes,
        compiler_params=pltpu.CompilerParams(vmem_limit_bytes=GRANT),
        cost_estimate=pl.CostEstimate(flops=flops, bytes_accessed=moved, transcendentals=0),
        name=name,
    )


def on_device(three_center, metric_tensor, density, pattern, block_size):
    funcs = three_center.shape[1] // WIDTH
    spread = density.T
    message = pltpu.VMEM((SIDE, (funcs + 1) * LANES), jnp.bfloat16)
    odd_up, even_up = call(
        pack_kernel,
        (message, message),
        [HBM] * 4,
        "pack_halo",
        0,
        1 << 20,
        [
            pltpu.VMEM(metric_tensor.shape, jnp.bfloat16),
            pltpu.VMEM(spread.shape, jnp.bfloat16),
            pltpu.SMEM(pattern.shape, jnp.int32),
            pltpu.SMEM(block_size.shape, jnp.int32),
            pltpu.SemaphoreType.DMA((3 + ATOMS,)),
        ],
    )(*[pltpu.with_memory_space_constraint(x, pltpu.HBM) for x in (metric_tensor, spread, pattern, block_size)])
    peers, funcs_at = lax.axis_size("orb"), lax.axis_size("aux")
    odd_pairs = [(i, (i + 1) % peers if i % 2 else (i - 1) % peers) for i in range(peers)]
    even_pairs = [(i, i + 1 if i % 2 == 0 else i - 1) for i in range(peers)]
    ahead = [(i + 1, i) for i in AHEAD]
    behind = [pair for pair in even_pairs if pair not in ahead]

    def swap(message, *pairs_of_core):
        pairs = [
            (i * funcs_at + z, j * funcs_at + z) for z in range(funcs_at) for i, j in pairs_of_core[z % 2]
        ]
        return lax.ppermute(message, ("orb", "aux"), pairs)

    from_first_even = swap(even_up, ahead, even_pairs)
    from_odd_up = swap(odd_up, odd_pairs, odd_pairs)
    from_even_up = swap(even_up, behind, [])
    wide = jax.ShapeDtypeStruct((funcs, ROWS, WINDOW), jnp.bfloat16)
    prepared = call(
        prepare_kernel,
        (
            wide,
            jax.ShapeDtypeStruct((ROWS, funcs * WINDOW), jnp.bfloat16),
            jax.ShapeDtypeStruct((WINDOW, WINDOW), jnp.bfloat16),
            jax.ShapeDtypeStruct((ROWS, WINDOW), jnp.bfloat16),
            message,
        ),
        [VMEM, VMEM, VMEM, SMEM, SMEM, VMEM],
        "window_layout",
        0,
        2 << 20,
    )(three_center, metric_tensor, spread, pattern, block_size, from_first_even)
    lead = funcs_at - 3
    order = [lead] + [i for i in range(funcs_at) if i != lead]
    partial_sum = call(
        functools.partial(main_kernel, [order.index(i) for i in range(funcs_at)]),
        jax.ShapeDtypeStruct((ROWS // 8, 8, WIDTH), jnp.bfloat16),
        [VMEM] * 7,
        "exchange_terms",
        1 << 28,
        2 << 20,
        [pltpu.VMEM((WINDOW, WINDOW), jnp.bfloat16)],
    )(*prepared, from_odd_up, from_even_up)
    terms = lax.all_to_all(partial_sum, "aux", 0, 0, axis_index_groups=[order])
    return jnp.sum(terms.astype(jnp.float32), axis=0).astype(jnp.bfloat16)


def solution(mesh):
    placed = (P("orb", "aux"), P("orb", "aux"), P("orb", None), P("orb", None), P())
    return jax.shard_map(
        on_device, mesh=mesh, in_specs=placed, out_specs=P(("orb", "aux"), None), check_vma=False
    )
```

```python
import functools

import jax
import jax.numpy as jnp
from jax import lax
from jax.experimental import pallas as pl
from jax.experimental.pallas import tpu as pltpu
from jax.sharding import PartitionSpec as P

BS = 16
HALF = 4
SLOTS = 2 * HALF + 1
WIDTH = SLOTS * BS
ATOMS = 8
ROWS = ATOMS * BS
SIDE = HALF * BS
WINDOW = (ATOMS + 2 * HALF) * BS
LANES = 128
PER = LANES // BS
VMEM = pl.BlockSpec(memory_space=pltpu.VMEM)
SMEM = pl.BlockSpec(memory_space=pltpu.SMEM)
HBM = pl.BlockSpec(memory_space=pltpu.HBM)
GRANT = 8 * 1024 * 1024
NT = (((1,), (1,)), ((), ()))
AHEAD = (0, 20, 24, 28)


def iota(shape, dim):
    return lax.broadcasted_iota(jnp.int32, shape, dim)


def window_sizes(size_ref):
    total = size_ref.shape[0]
    first = lax.axis_index("orb") * ATOMS + total - HALF
    return [size_ref[lax.rem(first + c, total)] for c in range(ATOMS + 2 * HALF)]


def by_group(values):
    group = iota((8, LANES), 1) // BS
    out = jnp.zeros((8, LANES), jnp.int32)
    for g, value in values.items():
        out = jnp.where(group == g, value, out)
    return out


def row_mask(pattern_ref, sizes, a, first):
    limit = by_group(
        {
            c - first: pattern_ref[a, c - a] * sizes[c]
            for c in range(first, first + PER)
            if 0 <= c - a < SLOTS
        }
    )
    func = iota((8, LANES), 1) % BS
    row = iota((8, LANES), 0)
    size = sizes[a + HALF]
    halves = [jnp.where((func < limit) & (row + 8 * h < size), 1.0, 0.0) for h in range(2)]
    return jnp.concatenate(halves, axis=0).astype(jnp.bfloat16)


def banded(ref, rows, start, shift, count):
    base = start - shift
    low = base // LANES
    off = base - low * LANES
    last = ref.shape[1] // LANES
    need = count + (1 if off else 0)
    tiles = []
    for i in range(low, low + need):
        i = min(max(i, 0), last - 1)
        tiles.append(ref[rows, i * LANES : (i + 1) * LANES])
    if off:
        rolled = [pltpu.roll(t, LANES - off, 1) for t in tiles]
        lane = iota((BS, LANES), 1)
        tiles = [jnp.where(lane < LANES - off, rolled[i], rolled[i + 1]) for i in range(count)]
    return tiles


def density_rows(spread_ref, pattern_ref, sizes, slot_of, c):
    group = iota((BS, LANES), 1) // BS
    tile = jnp.zeros((BS, LANES), jnp.bfloat16)
    limits = {}
    for j, k in slot_of.items():
        tile = jnp.where(group == j, spread_ref[k * BS : (k + 1) * BS, :], tile)
        limits[j] = pattern_ref[j, k] * sizes[c[j]]
    limit = by_group(limits)
    own = by_group({j: sizes[j + HALF] for j in slot_of})
    live = iota((8, LANES), 1) % BS < own
    row = iota((8, LANES), 0)
    halves = [jnp.where((row + 8 * h < limit) & live, 1.0, 0.0) for h in range(2)]
    return tile * jnp.concatenate(halves, axis=0).astype(jnp.bfloat16)


def pack_halo(metric_ref, spread_ref, pattern_ref, sizes, up_ref, down_ref):
    lane = iota((BS, LANES), 1)
    density = []
    for g in range(PER):
        slot_of, atom_of = {}, {}
        for j in range(ATOMS):
            at = g if j < HALF else g + ATOMS
            if 0 <= at - j < SLOTS:
                slot_of[j], atom_of[j] = at - j, at
        density.append(density_rows(spread_ref, pattern_ref, sizes, slot_of, atom_of))
    for a in range(ATOMS):
        rows = slice(a * BS, (a + 1) * BS)
        first = 0 if a < HALF else ATOMS
        out_ref = down_ref if a < HALF else up_ref
        out_rows = slice((a % HALF) * BS, (a % HALF + 1) * BS)
        mask = row_mask(pattern_ref, sizes, a, first)
        for p in range(PER):
            tile = banded(metric_ref, rows, p * WIDTH, (a - first) * BS, 1)[0] * mask
            if a == 2:
                tile = jnp.where(lane < 16, pltpu.roll(density[p], 80, 1), tile)
            elif a == 3:
                tile = jnp.where(lane < 48, density[p], tile)
            elif a == 4:
                tile = jnp.where(lane >= 80, density[p], tile)
            elif a == 5:
                tile = jnp.where((lane >= 96) & (lane < 112), pltpu.roll(density[p], 32, 1), tile)
            out_ref[out_rows, p * LANES : (p + 1) * LANES] = tile


def pack_kernel(
    metric_hbm,
    spread_hbm,
    pattern_hbm,
    size_hbm,
    odd_up_ref,
    even_up_ref,
    metric_ref,
    spread_ref,
    pattern_ref,
    size_ref,
    sems,
):
    blocks = [pl.ds(a * BS, BS) for a in range(ATOMS)]
    pairs = (
        (size_hbm, size_ref),
        (pattern_hbm, pattern_ref),
        (spread_hbm, spread_ref),
        *((metric_hbm.at[rows], metric_ref.at[rows]) for rows in blocks),
    )
    copies = [pltpu.make_async_copy(src, dst, sems.at[i]) for i, (src, dst) in enumerate(pairs)]
    for copy in copies:
        copy.start()
    for copy in copies:
        copy.wait()
    sizes = window_sizes(size_ref)
    odd = lax.rem(lax.axis_index("orb"), 2) == 1

    @pl.when(odd)
    def _():
        pack_halo(metric_ref, spread_ref, pattern_ref, sizes, odd_up_ref, even_up_ref)

    @pl.when(jnp.logical_not(odd))
    def _():
        pack_halo(metric_ref, spread_ref, pattern_ref, sizes, even_up_ref, odd_up_ref)


def prepare_kernel(
    three_ref,
    metric_ref,
    spread_ref,
    pattern_ref,
    size_ref,
    message_ref,
    three_win,
    metric_win,
    spread_win,
    kept_win,
    first_ref,
):
    first_ref[...] = message_ref[...]
    sizes = window_sizes(size_ref)
    funcs = metric_ref.shape[1] // WIDTH
    for a in range(ATOMS):
        rows = slice(a * BS, (a + 1) * BS)
        masks = [row_mask(pattern_ref, sizes, a, h * PER) for h in range(2)]
        for h in range(2):
            kept_win[rows, h * LANES : (h + 1) * LANES] = masks[h]
        for p in range(funcs):
            tiles = banded(three_ref, rows, p * WIDTH, a * BS, 2)
            for h in range(2):
                three_win[p, rows, h * LANES : (h + 1) * LANES] = tiles[h] * masks[h]
            tiles = banded(metric_ref, rows, p * WIDTH, a * BS, 2)
            for h in range(2):
                cols = slice(p * WINDOW + h * LANES, p * WINDOW + (h + 1) * LANES)
                metric_win[rows, cols] = tiles[h] * masks[h]
    lane = iota((BS, LANES), 1)
    zero = jnp.zeros((BS, LANES), jnp.bfloat16)
    for c in range(ATOMS + 2 * HALF):
        slot_of = {j: c - j for j in range(ATOMS) if 0 <= c - j < SLOTS}
        tile = density_rows(spread_ref, pattern_ref, sizes, slot_of, {j: c for j in slot_of})
        tile = pltpu.roll(tile, LANES // 2, 1)
        rows = slice(c * BS, (c + 1) * BS)
        spread_win[rows, :LANES] = jnp.where(lane < LANES // 2, zero, tile)
        spread_win[rows, LANES:] = jnp.where(lane < LANES // 2, tile, zero)


def main_kernel(place, three_win, metric_win, spread_win, kept_win, first_ref, odd_up_ref, even_up_ref, out_ref, spread_all):
    funcs = three_win.shape[0]
    lane = iota((BS, LANES), 1)
    odd = lax.rem(lax.axis_index("orb"), 2) == 1
    here = lax.axis_index("orb")
    is_first = lax.rem(lax.axis_index("aux"), 2) == 1
    for target in AHEAD:
        is_first |= here == target

    def tiles_of(i, p):
        place = slice(i * BS, (i + 1) * BS), slice(p * LANES, (p + 1) * LANES)
        even = jnp.where(is_first, first_ref[place], even_up_ref[place])
        other = odd_up_ref[place]
        return jnp.where(odd, even, other), jnp.where(odd, other, even)

    before, after = [], []
    for i in range(HALF):
        tiles = [tiles_of(i, p) for p in range(funcs)]
        before.append([t[0] for t in tiles])
        after.append([t[1] for t in tiles])
    spread_all[...] = spread_win[...]
    for g in range(PER):
        rows = slice(g * BS, (g + 1) * BS)
        own = spread_win[rows, :LANES]
        tile = jnp.where(lane < LANES // 2, pltpu.roll(before[0][g], 64, 1), own)
        spread_all[rows, :LANES] = jnp.where(lane < BS, pltpu.roll(before[1][g], 32, 1), tile)
        rows = slice((PER + g) * BS, (PER + g + 1) * BS)
        own = spread_win[rows, LANES:]
        tile = jnp.where(lane >= LANES // 2, pltpu.roll(after[3][g], 64, 1), own)
        spread_all[rows, LANES:] = jnp.where(lane >= LANES - BS, pltpu.roll(after[2][g], 112, 1), tile)
    zero = jnp.zeros((BS, LANES), jnp.bfloat16)
    side_rows = []
    for i in range(HALF):
        side_rows.append([jnp.where(lane < (i + HALF + 1) * BS, t, zero) if i < 2 else t for t in before[i]])
    for i in range(HALF):
        side_rows.append([jnp.where(lane >= i * BS, t, zero) if i >= 2 else t for t in after[i]])
    atom = iota((ROWS, WINDOW), 0) // BS
    slot = iota((ROWS, WINDOW), 1) // BS - atom
    in_band = (slot >= 0) & (slot < SLOTS)
    spread = lax.dot_general(
        three_win[...].reshape(funcs * ROWS, WINDOW), spread_all[...], NT, preferred_element_type=jnp.float32
    )
    contracted = [
        jnp.where(in_band, spread[p * ROWS : (p + 1) * ROWS], 0.0).astype(jnp.bfloat16) for p in range(funcs)
    ]
    own = lax.dot_general(
        jnp.concatenate(contracted, axis=1), metric_win[...], NT, preferred_element_type=jnp.float32
    )
    near = [jnp.concatenate([c[:SIDE, :LANES], c[SIDE:, LANES:]], axis=0) for c in contracted]
    sides = lax.dot_general(
        jnp.concatenate(near, axis=1),
        jnp.concatenate([jnp.concatenate(block, axis=1) for block in side_rows], axis=0),
        NT,
        preferred_element_type=jnp.float32,
    )
    total = jnp.concatenate([sides[:, :SIDE], own, sides[:, SIDE:]], axis=1)
    total = jnp.where(kept_win[...] > 0, total, 0.0)
    for a in range(ATOMS):
        block = total[a * BS : (a + 1) * BS]
        block = pltpu.roll(block, WINDOW - a * BS, 1) if a else block
        for h in range(2):
            out_ref[place[2 * a + h]] = block[h * 8 : (h + 1) * 8, :WIDTH].astype(jnp.bfloat16)


def call(kernel, out_shape, in_specs, name, flops=0, moved=0, scratch_shapes=()):
    return pl.pallas_call(
        kernel,
        out_shape=out_shape,
        in_specs=in_specs,
        out_specs=(VMEM,) * len(out_shape) if isinstance(out_shape, tuple) else VMEM,
        scratch_shapes=scratch_shapes,
        compiler_params=pltpu.CompilerParams(vmem_limit_bytes=GRANT),
        cost_estimate=pl.CostEstimate(flops=flops, bytes_accessed=moved, transcendentals=0),
        name=name,
    )


def on_device(three_center, metric_tensor, density, pattern, block_size):
    funcs = three_center.shape[1] // WIDTH
    spread = density.T
    message = pltpu.VMEM((SIDE, funcs * LANES), jnp.bfloat16)
    odd_up, even_up = call(
        pack_kernel,
        (message, message),
        [HBM] * 4,
        "pack_halo",
        0,
        1 << 20,
        [
            pltpu.VMEM(metric_tensor.shape, jnp.bfloat16),
            pltpu.VMEM(spread.shape, jnp.bfloat16),
            pltpu.SMEM(pattern.shape, jnp.int32),
            pltpu.SMEM(block_size.shape, jnp.int32),
            pltpu.SemaphoreType.DMA((3 + ATOMS,)),
        ],
    )(*[pltpu.with_memory_space_constraint(x, pltpu.HBM) for x in (metric_tensor, spread, pattern, block_size)])
    peers, funcs_at = lax.axis_size("orb"), lax.axis_size("aux")
    odd_pairs = [(i, (i + 1) % peers if i % 2 else (i - 1) % peers) for i in range(peers)]
    even_pairs = [(i, i + 1 if i % 2 == 0 else i - 1) for i in range(peers)]
    ahead = [(i + 1, i) for i in AHEAD]
    behind = [pair for pair in even_pairs if pair not in ahead]

    def swap(message, *pairs_of_core):
        pairs = [
            (i * funcs_at + z, j * funcs_at + z) for z in range(funcs_at) for i, j in pairs_of_core[z % 2]
        ]
        return lax.ppermute(message, ("orb", "aux"), pairs)

    from_first_even = swap(even_up, ahead, even_pairs)
    from_odd_up = swap(odd_up, odd_pairs, odd_pairs)
    from_even_up = swap(even_up, behind, [])
    wide = jax.ShapeDtypeStruct((funcs, ROWS, WINDOW), jnp.bfloat16)
    prepared = call(
        prepare_kernel,
        (
            wide,
            jax.ShapeDtypeStruct((ROWS, funcs * WINDOW), jnp.bfloat16),
            jax.ShapeDtypeStruct((WINDOW, WINDOW), jnp.bfloat16),
            jax.ShapeDtypeStruct((ROWS, WINDOW), jnp.bfloat16),
            message,
        ),
        [VMEM, VMEM, VMEM, SMEM, SMEM, VMEM],
        "window_layout",
        0,
        2 << 20,
    )(three_center, metric_tensor, spread, pattern, block_size, from_first_even)
    lead = funcs_at - 3
    order = [lead] + [i for i in range(funcs_at) if i != lead]
    partial_sum = call(
        functools.partial(main_kernel, [order.index(i) for i in range(funcs_at)]),
        jax.ShapeDtypeStruct((ROWS // 8, 8, WIDTH), jnp.bfloat16),
        [VMEM] * 7,
        "exchange_terms",
        1 << 28,
        2 << 20,
        [pltpu.VMEM((WINDOW, WINDOW), jnp.bfloat16)],
    )(*prepared, from_odd_up, from_even_up)
    terms = lax.all_to_all(partial_sum, "aux", 0, 0, axis_index_groups=[order])
    return jnp.sum(terms.astype(jnp.float32), axis=0).astype(jnp.bfloat16)


def solution(mesh):
    placed = (P("orb", "aux"), P("orb", "aux"), P("orb", None), P("orb", None), P())
    return jax.shard_map(
        on_device, mesh=mesh, in_specs=placed, out_specs=P(("orb", "aux"), None), check_vma=False
    )
```

```python
import functools

import jax
import jax.numpy as jnp
from jax import lax
from jax.experimental import pallas as pl
from jax.experimental.pallas import tpu as pltpu
from jax.sharding import PartitionSpec as P

BS = 16
HALF = 4
SLOTS = 2 * HALF + 1
WIDTH = SLOTS * BS
ATOMS = 8
ROWS = ATOMS * BS
SIDE = HALF * BS
WINDOW = (ATOMS + 2 * HALF) * BS
LANES = 128
PER = LANES // BS
VMEM = pl.BlockSpec(memory_space=pltpu.VMEM)
SMEM = pl.BlockSpec(memory_space=pltpu.SMEM)
HBM = pl.BlockSpec(memory_space=pltpu.HBM)
GRANT = 8 * 1024 * 1024
NT = (((1,), (1,)), ((), ()))
AHEAD = (0, 20, 24, 28)


def iota(shape, dim):
    return lax.broadcasted_iota(jnp.int32, shape, dim)


def window_sizes(size_ref):
    total = size_ref.shape[0]
    first = lax.axis_index("orb") * ATOMS + total - HALF
    return [size_ref[lax.rem(first + c, total)] for c in range(ATOMS + 2 * HALF)]


def by_group(values):
    group = iota((8, LANES), 1) // BS
    out = jnp.zeros((8, LANES), jnp.int32)
    for g, value in values.items():
        out = jnp.where(group == g, value, out)
    return out


def row_mask(pattern_ref, sizes, a, first):
    limit = by_group(
        {
            c - first: pattern_ref[a, c - a] * sizes[c]
            for c in range(first, first + PER)
            if 0 <= c - a < SLOTS
        }
    )
    func = iota((8, LANES), 1) % BS
    row = iota((8, LANES), 0)
    size = sizes[a + HALF]
    halves = [jnp.where((func < limit) & (row + 8 * h < size), 1.0, 0.0) for h in range(2)]
    return jnp.concatenate(halves, axis=0).astype(jnp.bfloat16)


def banded(ref, rows, start, shift, count):
    base = start - shift
    low = base // LANES
    off = base - low * LANES
    last = ref.shape[1] // LANES
    need = count + (1 if off else 0)
    tiles = []
    for i in range(low, low + need):
        i = min(max(i, 0), last - 1)
        tiles.append(ref[rows, i * LANES : (i + 1) * LANES])
    if off:
        rolled = [pltpu.roll(t, LANES - off, 1) for t in tiles]
        lane = iota((BS, LANES), 1)
        tiles = [jnp.where(lane < LANES - off, rolled[i], rolled[i + 1]) for i in range(count)]
    return tiles


def density_rows(spread_ref, pattern_ref, sizes, slot_of, c):
    group = iota((BS, LANES), 1) // BS
    tile = jnp.zeros((BS, LANES), jnp.bfloat16)
    limits = {}
    for j, k in slot_of.items():
        tile = jnp.where(group == j, spread_ref[k * BS : (k + 1) * BS, :], tile)
        limits[j] = pattern_ref[j, k] * sizes[c[j]]
    limit = by_group(limits)
    own = by_group({j: sizes[j + HALF] for j in slot_of})
    live = iota((8, LANES), 1) % BS < own
    row = iota((8, LANES), 0)
    halves = [jnp.where((row + 8 * h < limit) & live, 1.0, 0.0) for h in range(2)]
    return tile * jnp.concatenate(halves, axis=0).astype(jnp.bfloat16)


def pack_halo(metric_ref, spread_ref, pattern_ref, sizes, up_ref, down_ref):
    lane = iota((BS, LANES), 1)
    density = []
    for g in range(PER):
        slot_of, atom_of = {}, {}
        for j in range(ATOMS):
            at = g if j < HALF else g + ATOMS
            if 0 <= at - j < SLOTS:
                slot_of[j], atom_of[j] = at - j, at
        density.append(density_rows(spread_ref, pattern_ref, sizes, slot_of, atom_of))
    for a in range(ATOMS):
        rows = slice(a * BS, (a + 1) * BS)
        first = 0 if a < HALF else ATOMS
        out_ref = down_ref if a < HALF else up_ref
        out_rows = slice((a % HALF) * BS, (a % HALF + 1) * BS)
        mask = row_mask(pattern_ref, sizes, a, first)
        for p in range(PER):
            tile = banded(metric_ref, rows, p * WIDTH, (a - first) * BS, 1)[0] * mask
            if a == 2:
                tile = jnp.where(lane < 16, pltpu.roll(density[p], 80, 1), tile)
            elif a == 3:
                tile = jnp.where(lane < 48, density[p], tile)
            elif a == 4:
                tile = jnp.where(lane >= 80, density[p], tile)
            elif a == 5:
                tile = jnp.where((lane >= 96) & (lane < 112), pltpu.roll(density[p], 32, 1), tile)
            out_ref[out_rows, p * LANES : (p + 1) * LANES] = tile


def pack_kernel(
    metric_hbm,
    spread_hbm,
    pattern_hbm,
    size_hbm,
    odd_up_ref,
    even_up_ref,
    metric_ref,
    spread_ref,
    pattern_ref,
    size_ref,
    sems,
):
    blocks = [pl.ds(a * BS, BS) for a in range(ATOMS)]
    pairs = (
        (size_hbm, size_ref),
        (pattern_hbm, pattern_ref),
        (spread_hbm, spread_ref),
        *((metric_hbm.at[rows], metric_ref.at[rows]) for rows in blocks),
    )
    copies = [pltpu.make_async_copy(src, dst, sems.at[i]) for i, (src, dst) in enumerate(pairs)]
    for copy in copies:
        copy.start()
    for copy in copies:
        copy.wait()
    sizes = window_sizes(size_ref)
    odd = lax.rem(lax.axis_index("orb"), 2) == 1

    @pl.when(odd)
    def _():
        pack_halo(metric_ref, spread_ref, pattern_ref, sizes, odd_up_ref, even_up_ref)

    @pl.when(jnp.logical_not(odd))
    def _():
        pack_halo(metric_ref, spread_ref, pattern_ref, sizes, even_up_ref, odd_up_ref)


def prepare_kernel(
    three_ref,
    metric_ref,
    spread_ref,
    pattern_ref,
    size_ref,
    message_ref,
    three_win,
    metric_win,
    spread_win,
    kept_win,
    first_ref,
):
    first_ref[...] = message_ref[...]
    sizes = window_sizes(size_ref)
    funcs = metric_ref.shape[1] // WIDTH
    for a in range(ATOMS):
        rows = slice(a * BS, (a + 1) * BS)
        masks = [row_mask(pattern_ref, sizes, a, h * PER) for h in range(2)]
        for h in range(2):
            kept_win[rows, h * LANES : (h + 1) * LANES] = masks[h]
        for p in range(funcs):
            tiles = banded(three_ref, rows, p * WIDTH, a * BS, 2)
            for h in range(2):
                three_win[p, rows, h * LANES : (h + 1) * LANES] = tiles[h] * masks[h]
            tiles = banded(metric_ref, rows, p * WIDTH, a * BS, 2)
            for h in range(2):
                cols = slice(p * WINDOW + h * LANES, p * WINDOW + (h + 1) * LANES)
                metric_win[rows, cols] = tiles[h] * masks[h]
    lane = iota((BS, LANES), 1)
    zero = jnp.zeros((BS, LANES), jnp.bfloat16)
    for c in range(ATOMS + 2 * HALF):
        slot_of = {j: c - j for j in range(ATOMS) if 0 <= c - j < SLOTS}
        tile = density_rows(spread_ref, pattern_ref, sizes, slot_of, {j: c for j in slot_of})
        tile = pltpu.roll(tile, LANES // 2, 1)
        rows = slice(c * BS, (c + 1) * BS)
        spread_win[rows, :LANES] = jnp.where(lane < LANES // 2, zero, tile)
        spread_win[rows, LANES:] = jnp.where(lane < LANES // 2, tile, zero)


def main_kernel(place, three_win, metric_win, spread_win, kept_win, first_ref, odd_up_ref, even_up_ref, out_ref, spread_all):
    funcs = three_win.shape[0]
    lane = iota((BS, LANES), 1)
    odd = lax.rem(lax.axis_index("orb"), 2) == 1
    here = lax.axis_index("orb")
    is_first = (lax.rem(lax.axis_index("aux"), 2) == 1) & (here < lax.axis_size("orb") - 2)
    for target in AHEAD:
        is_first |= here == target

    def tiles_of(i, p):
        place = slice(i * BS, (i + 1) * BS), slice(p * LANES, (p + 1) * LANES)
        even = jnp.where(is_first, first_ref[place], even_up_ref[place])
        other = odd_up_ref[place]
        return jnp.where(odd, even, other), jnp.where(odd, other, even)

    before, after = [], []
    for i in range(HALF):
        tiles = [tiles_of(i, p) for p in range(funcs)]
        before.append([t[0] for t in tiles])
        after.append([t[1] for t in tiles])
    spread_all[...] = spread_win[...]
    for g in range(PER):
        rows = slice(g * BS, (g + 1) * BS)
        own = spread_win[rows, :LANES]
        tile = jnp.where(lane < LANES // 2, pltpu.roll(before[0][g], 64, 1), own)
        spread_all[rows, :LANES] = jnp.where(lane < BS, pltpu.roll(before[1][g], 32, 1), tile)
        rows = slice((PER + g) * BS, (PER + g + 1) * BS)
        own = spread_win[rows, LANES:]
        tile = jnp.where(lane >= LANES // 2, pltpu.roll(after[3][g], 64, 1), own)
        spread_all[rows, LANES:] = jnp.where(lane >= LANES - BS, pltpu.roll(after[2][g], 112, 1), tile)
    zero = jnp.zeros((BS, LANES), jnp.bfloat16)
    side_rows = []
    for i in range(HALF):
        side_rows.append([jnp.where(lane < (i + HALF + 1) * BS, t, zero) if i < 2 else t for t in before[i]])
    for i in range(HALF):
        side_rows.append([jnp.where(lane >= i * BS, t, zero) if i >= 2 else t for t in after[i]])
    atom = iota((ROWS, WINDOW), 0) // BS
    slot = iota((ROWS, WINDOW), 1) // BS - atom
    in_band = (slot >= 0) & (slot < SLOTS)
    spread = lax.dot_general(
        three_win[...].reshape(funcs * ROWS, WINDOW), spread_all[...], NT, preferred_element_type=jnp.float32
    )
    contracted = [
        jnp.where(in_band, spread[p * ROWS : (p + 1) * ROWS], 0.0).astype(jnp.bfloat16) for p in range(funcs)
    ]
    own = lax.dot_general(
        jnp.concatenate(contracted, axis=1), metric_win[...], NT, preferred_element_type=jnp.float32
    )
    near = [jnp.concatenate([c[:SIDE, :LANES], c[SIDE:, LANES:]], axis=0) for c in contracted]
    sides = lax.dot_general(
        jnp.concatenate(near, axis=1),
        jnp.concatenate([jnp.concatenate(block, axis=1) for block in side_rows], axis=0),
        NT,
        preferred_element_type=jnp.float32,
    )
    total = jnp.concatenate([sides[:, :SIDE], own, sides[:, SIDE:]], axis=1)
    total = jnp.where(kept_win[...] > 0, total, 0.0)
    for a in range(ATOMS):
        block = total[a * BS : (a + 1) * BS]
        block = pltpu.roll(block, WINDOW - a * BS, 1) if a else block
        for h in range(2):
            out_ref[place[2 * a + h]] = block[h * 8 : (h + 1) * 8, :WIDTH].astype(jnp.bfloat16)


def call(kernel, out_shape, in_specs, name, flops=0, moved=0, scratch_shapes=()):
    return pl.pallas_call(
        kernel,
        out_shape=out_shape,
        in_specs=in_specs,
        out_specs=(VMEM,) * len(out_shape) if isinstance(out_shape, tuple) else VMEM,
        scratch_shapes=scratch_shapes,
        compiler_params=pltpu.CompilerParams(vmem_limit_bytes=GRANT),
        cost_estimate=pl.CostEstimate(flops=flops, bytes_accessed=moved, transcendentals=0),
        name=name,
    )


def on_device(three_center, metric_tensor, density, pattern, block_size):
    funcs = three_center.shape[1] // WIDTH
    spread = density.T
    message = pltpu.VMEM((SIDE, funcs * LANES), jnp.bfloat16)
    odd_up, even_up = call(
        pack_kernel,
        (message, message),
        [HBM] * 4,
        "pack_halo",
        0,
        1 << 20,
        [
            pltpu.VMEM(metric_tensor.shape, jnp.bfloat16),
            pltpu.VMEM(spread.shape, jnp.bfloat16),
            pltpu.SMEM(pattern.shape, jnp.int32),
            pltpu.SMEM(block_size.shape, jnp.int32),
            pltpu.SemaphoreType.DMA((3 + ATOMS,)),
        ],
    )(*[pltpu.with_memory_space_constraint(x, pltpu.HBM) for x in (metric_tensor, spread, pattern, block_size)])
    peers, funcs_at = lax.axis_size("orb"), lax.axis_size("aux")
    odd_pairs = [(i, (i + 1) % peers if i % 2 else (i - 1) % peers) for i in range(peers)]
    even_pairs = [(i, i + 1 if i % 2 == 0 else i - 1) for i in range(peers)]
    ahead = [(i + 1, i) for i in AHEAD]
    behind = [pair for pair in even_pairs if pair not in ahead]

    def swap(message, *pairs_of_core):
        pairs = [
            (i * funcs_at + z, j * funcs_at + z) for z in range(funcs_at) for i, j in pairs_of_core[z % 2]
        ]
        return lax.ppermute(message, ("orb", "aux"), pairs)

    late = [(i, j) for i, j in even_pairs if peers - 1 in (i, j)]
    from_first_even = swap(even_up, ahead, [p for p in even_pairs if p not in late])
    from_odd_up = swap(odd_up, odd_pairs, odd_pairs)
    from_even_up = swap(even_up, behind, late)
    wide = jax.ShapeDtypeStruct((funcs, ROWS, WINDOW), jnp.bfloat16)
    prepared = call(
        prepare_kernel,
        (
            wide,
            jax.ShapeDtypeStruct((ROWS, funcs * WINDOW), jnp.bfloat16),
            jax.ShapeDtypeStruct((WINDOW, WINDOW), jnp.bfloat16),
            jax.ShapeDtypeStruct((ROWS, WINDOW), jnp.bfloat16),
            message,
        ),
        [VMEM, VMEM, VMEM, SMEM, SMEM, VMEM],
        "window_layout",
        0,
        2 << 20,
    )(three_center, metric_tensor, spread, pattern, block_size, from_first_even)
    lead = funcs_at - 3
    order = [lead] + [i for i in range(funcs_at) if i != lead]
    partial_sum = call(
        functools.partial(main_kernel, [order.index(i) for i in range(funcs_at)]),
        jax.ShapeDtypeStruct((ROWS // 8, 8, WIDTH), jnp.bfloat16),
        [VMEM] * 7,
        "exchange_terms",
        1 << 28,
        2 << 20,
        [pltpu.VMEM((WINDOW, WINDOW), jnp.bfloat16)],
    )(*prepared, from_odd_up, from_even_up)
    terms = lax.all_to_all(partial_sum, "aux", 0, 0, axis_index_groups=[order])
    return jnp.sum(terms.astype(jnp.float32), axis=0).astype(jnp.bfloat16)


def solution(mesh):
    placed = (P("orb", "aux"), P("orb", "aux"), P("orb", None), P("orb", None), P())
    return jax.shard_map(
        on_device, mesh=mesh, in_specs=placed, out_specs=P(("orb", "aux"), None), check_vma=False
    )
```

```python
import functools

import jax
import jax.numpy as jnp
from jax import lax
from jax.experimental import pallas as pl
from jax.experimental.pallas import tpu as pltpu
from jax.sharding import PartitionSpec as P

BS = 16
HALF = 4
SLOTS = 2 * HALF + 1
WIDTH = SLOTS * BS
ATOMS = 8
ROWS = ATOMS * BS
SIDE = HALF * BS
WINDOW = (ATOMS + 2 * HALF) * BS
LANES = 128
PER = LANES // BS
VMEM = pl.BlockSpec(memory_space=pltpu.VMEM)
SMEM = pl.BlockSpec(memory_space=pltpu.SMEM)
HBM = pl.BlockSpec(memory_space=pltpu.HBM)
GRANT = 8 * 1024 * 1024
NT = (((1,), (1,)), ((), ()))
AHEAD = (0, 20, 24, 28)


def iota(shape, dim):
    return lax.broadcasted_iota(jnp.int32, shape, dim)


def window_sizes(size_ref):
    total = size_ref.shape[0]
    first = lax.axis_index("orb") * ATOMS + total - HALF
    return [size_ref[lax.rem(first + c, total)] for c in range(ATOMS + 2 * HALF)]


def by_group(values):
    group = iota((8, LANES), 1) // BS
    out = jnp.zeros((8, LANES), jnp.int32)
    for g, value in values.items():
        out = jnp.where(group == g, value, out)
    return out


def row_mask(pattern_ref, sizes, a, first):
    limit = by_group(
        {
            c - first: pattern_ref[a, c - a] * sizes[c]
            for c in range(first, first + PER)
            if 0 <= c - a < SLOTS
        }
    )
    func = iota((8, LANES), 1) % BS
    row = iota((8, LANES), 0)
    size = sizes[a + HALF]
    halves = [jnp.where((func < limit) & (row + 8 * h < size), 1.0, 0.0) for h in range(2)]
    return jnp.concatenate(halves, axis=0).astype(jnp.bfloat16)


def banded(ref, rows, start, shift, count):
    base = start - shift
    low = base // LANES
    off = base - low * LANES
    last = ref.shape[1] // LANES
    need = count + (1 if off else 0)
    tiles = []
    for i in range(low, low + need):
        i = min(max(i, 0), last - 1)
        tiles.append(ref[rows, i * LANES : (i + 1) * LANES])
    if off:
        rolled = [pltpu.roll(t, LANES - off, 1) for t in tiles]
        lane = iota((BS, LANES), 1)
        tiles = [jnp.where(lane < LANES - off, rolled[i], rolled[i + 1]) for i in range(count)]
    return tiles


def density_rows(spread_ref, pattern_ref, sizes, slot_of, c):
    group = iota((BS, LANES), 1) // BS
    tile = jnp.zeros((BS, LANES), jnp.bfloat16)
    limits = {}
    for j, k in slot_of.items():
        tile = jnp.where(group == j, spread_ref[k * BS : (k + 1) * BS, :], tile)
        limits[j] = pattern_ref[j, k] * sizes[c[j]]
    limit = by_group(limits)
    own = by_group({j: sizes[j + HALF] for j in slot_of})
    live = iota((8, LANES), 1) % BS < own
    row = iota((8, LANES), 0)
    halves = [jnp.where((row + 8 * h < limit) & live, 1.0, 0.0) for h in range(2)]
    return tile * jnp.concatenate(halves, axis=0).astype(jnp.bfloat16)


def pack_halo(metric_ref, spread_ref, pattern_ref, sizes, up_ref, down_ref):
    lane = iota((BS, LANES), 1)
    density = []
    for g in range(PER):
        slot_of, atom_of = {}, {}
        for j in range(ATOMS):
            at = g if j < HALF else g + ATOMS
            if 0 <= at - j < SLOTS:
                slot_of[j], atom_of[j] = at - j, at
        density.append(density_rows(spread_ref, pattern_ref, sizes, slot_of, atom_of))
    for a in range(ATOMS):
        rows = slice(a * BS, (a + 1) * BS)
        first = 0 if a < HALF else ATOMS
        out_ref = down_ref if a < HALF else up_ref
        out_rows = slice((a % HALF) * BS, (a % HALF + 1) * BS)
        mask = row_mask(pattern_ref, sizes, a, first)
        for p in range(PER):
            tile = banded(metric_ref, rows, p * WIDTH, (a - first) * BS, 1)[0] * mask
            if a == 2:
                tile = jnp.where(lane < 16, pltpu.roll(density[p], 80, 1), tile)
            elif a == 3:
                tile = jnp.where(lane < 48, density[p], tile)
            elif a == 4:
                tile = jnp.where(lane >= 80, density[p], tile)
            elif a == 5:
                tile = jnp.where((lane >= 96) & (lane < 112), pltpu.roll(density[p], 32, 1), tile)
            out_ref[out_rows, p * LANES : (p + 1) * LANES] = tile


def pack_kernel(
    metric_hbm,
    spread_hbm,
    pattern_hbm,
    size_hbm,
    odd_up_ref,
    even_up_ref,
    metric_ref,
    spread_ref,
    pattern_ref,
    size_ref,
    sems,
):
    blocks = [pl.ds(a * BS, BS) for a in range(ATOMS)]
    pairs = (
        (size_hbm, size_ref),
        (pattern_hbm, pattern_ref),
        (spread_hbm, spread_ref),
        *((metric_hbm.at[rows], metric_ref.at[rows]) for rows in blocks),
    )
    copies = [pltpu.make_async_copy(src, dst, sems.at[i]) for i, (src, dst) in enumerate(pairs)]
    for copy in copies:
        copy.start()
    for copy in copies:
        copy.wait()
    sizes = window_sizes(size_ref)
    odd = lax.rem(lax.axis_index("orb"), 2) == 1

    @pl.when(odd)
    def _():
        pack_halo(metric_ref, spread_ref, pattern_ref, sizes, odd_up_ref, even_up_ref)

    @pl.when(jnp.logical_not(odd))
    def _():
        pack_halo(metric_ref, spread_ref, pattern_ref, sizes, even_up_ref, odd_up_ref)


def prepare_kernel(
    three_ref,
    metric_ref,
    spread_ref,
    pattern_ref,
    size_ref,
    message_ref,
    three_win,
    metric_win,
    spread_win,
    kept_win,
    first_ref,
):
    first_ref[...] = message_ref[...]
    sizes = window_sizes(size_ref)
    funcs = metric_ref.shape[1] // WIDTH
    for a in range(ATOMS):
        rows = slice(a * BS, (a + 1) * BS)
        masks = [row_mask(pattern_ref, sizes, a, h * PER) for h in range(2)]
        for h in range(2):
            kept_win[rows, h * LANES : (h + 1) * LANES] = masks[h]
        for p in range(funcs):
            tiles = banded(three_ref, rows, p * WIDTH, a * BS, 2)
            for h in range(2):
                three_win[p, rows, h * LANES : (h + 1) * LANES] = tiles[h] * masks[h]
            tiles = banded(metric_ref, rows, p * WIDTH, a * BS, 2)
            for h in range(2):
                cols = slice(p * WINDOW + h * LANES, p * WINDOW + (h + 1) * LANES)
                metric_win[rows, cols] = tiles[h] * masks[h]
    lane = iota((BS, LANES), 1)
    zero = jnp.zeros((BS, LANES), jnp.bfloat16)
    for c in range(ATOMS + 2 * HALF):
        slot_of = {j: c - j for j in range(ATOMS) if 0 <= c - j < SLOTS}
        tile = density_rows(spread_ref, pattern_ref, sizes, slot_of, {j: c for j in slot_of})
        tile = pltpu.roll(tile, LANES // 2, 1)
        rows = slice(c * BS, (c + 1) * BS)
        spread_win[rows, :LANES] = jnp.where(lane < LANES // 2, zero, tile)
        spread_win[rows, LANES:] = jnp.where(lane < LANES // 2, tile, zero)


def main_kernel(place, three_win, metric_win, spread_win, kept_win, first_ref, odd_up_ref, even_up_ref, out_ref, spread_all):
    funcs = three_win.shape[0]
    lane = iota((BS, LANES), 1)
    odd = lax.rem(lax.axis_index("orb"), 2) == 1
    here = lax.axis_index("orb")
    is_first = lax.rem(lax.axis_index("aux"), 2) == 1
    for target in AHEAD:
        is_first |= here == target

    def tiles_of(i, p):
        place = slice(i * BS, (i + 1) * BS), slice(p * LANES, (p + 1) * LANES)
        even = jnp.where(is_first, first_ref[place], even_up_ref[place])
        other = odd_up_ref[place]
        return jnp.where(odd, even, other), jnp.where(odd, other, even)

    before, after = [], []
    for i in range(HALF):
        tiles = [tiles_of(i, p) for p in range(funcs)]
        before.append([t[0] for t in tiles])
        after.append([t[1] for t in tiles])
    spread_all[...] = spread_win[...]
    for g in range(PER):
        rows = slice(g * BS, (g + 1) * BS)
        own = spread_win[rows, :LANES]
        tile = jnp.where(lane < LANES // 2, pltpu.roll(before[0][g], 64, 1), own)
        spread_all[rows, :LANES] = jnp.where(lane < BS, pltpu.roll(before[1][g], 32, 1), tile)
        rows = slice((PER + g) * BS, (PER + g + 1) * BS)
        own = spread_win[rows, LANES:]
        tile = jnp.where(lane >= LANES // 2, pltpu.roll(after[3][g], 64, 1), own)
        spread_all[rows, LANES:] = jnp.where(lane >= LANES - BS, pltpu.roll(after[2][g], 112, 1), tile)
    zero = jnp.zeros((BS, LANES), jnp.bfloat16)
    side_rows = []
    for i in range(HALF):
        side_rows.append([jnp.where(lane < (i + HALF + 1) * BS, t, zero) if i < 2 else t for t in before[i]])
    for i in range(HALF):
        side_rows.append([jnp.where(lane >= i * BS, t, zero) if i >= 2 else t for t in after[i]])
    atom = iota((ROWS, WINDOW), 0) // BS
    slot = iota((ROWS, WINDOW), 1) // BS - atom
    in_band = (slot >= 0) & (slot < SLOTS)
    spread = lax.dot_general(
        three_win[...].reshape(funcs * ROWS, WINDOW), spread_all[...], NT, preferred_element_type=jnp.float32
    )
    contracted = [
        jnp.where(in_band, spread[p * ROWS : (p + 1) * ROWS], 0.0).astype(jnp.bfloat16) for p in range(funcs)
    ]
    own = lax.dot_general(
        jnp.concatenate(contracted, axis=1), metric_win[...], NT, preferred_element_type=jnp.float32
    )
    near = [jnp.concatenate([c[:SIDE, :LANES], c[SIDE:, LANES:]], axis=0) for c in contracted]
    sides = lax.dot_general(
        jnp.concatenate(near, axis=1),
        jnp.concatenate([jnp.concatenate(block, axis=1) for block in side_rows], axis=0),
        NT,
        preferred_element_type=jnp.float32,
    )
    total = jnp.concatenate([sides[:, :SIDE], own, sides[:, SIDE:]], axis=1)
    total = jnp.where(kept_win[...] > 0, total, 0.0)
    for a in range(ATOMS):
        block = total[a * BS : (a + 1) * BS]
        block = pltpu.roll(block, WINDOW - a * BS, 1) if a else block
        for h in range(2):
            out_ref[place[2 * a + h]] = block[h * 8 : (h + 1) * 8, :WIDTH].astype(jnp.bfloat16)


def call(kernel, out_shape, in_specs, name, flops=0, moved=0, scratch_shapes=()):
    return pl.pallas_call(
        kernel,
        out_shape=out_shape,
        in_specs=in_specs,
        out_specs=(VMEM,) * len(out_shape) if isinstance(out_shape, tuple) else VMEM,
        scratch_shapes=scratch_shapes,
        compiler_params=pltpu.CompilerParams(vmem_limit_bytes=GRANT),
        cost_estimate=pl.CostEstimate(flops=flops, bytes_accessed=moved, transcendentals=0),
        name=name,
    )


def on_device(three_center, metric_tensor, density, pattern, block_size):
    funcs = three_center.shape[1] // WIDTH
    spread = density.T
    message = pltpu.VMEM((SIDE, funcs * LANES), jnp.bfloat16)
    odd_up, even_up = call(
        pack_kernel,
        (message, message),
        [HBM] * 4,
        "pack_halo",
        0,
        1 << 20,
        [
            pltpu.VMEM(metric_tensor.shape, jnp.bfloat16),
            pltpu.VMEM(spread.shape, jnp.bfloat16),
            pltpu.SMEM(pattern.shape, jnp.int32),
            pltpu.SMEM(block_size.shape, jnp.int32),
            pltpu.SemaphoreType.DMA((3 + ATOMS,)),
        ],
    )(*[pltpu.with_memory_space_constraint(x, pltpu.HBM) for x in (metric_tensor, spread, pattern, block_size)])
    peers, funcs_at = lax.axis_size("orb"), lax.axis_size("aux")
    odd_pairs = [(i, (i + 1) % peers if i % 2 else (i - 1) % peers) for i in range(peers)]
    even_pairs = [(i, i + 1 if i % 2 == 0 else i - 1) for i in range(peers)]
    ahead = [(i + 1, i) for i in AHEAD]
    behind = [pair for pair in even_pairs if pair not in ahead]

    def swap(message, *pairs_of_core):
        pairs = [
            (i * funcs_at + z, j * funcs_at + z) for z in range(funcs_at) for i, j in pairs_of_core[z % 2]
        ]
        return lax.ppermute(message, ("orb", "aux"), pairs)

    from_first_even = swap(even_up, ahead, even_pairs)
    from_odd_up = swap(odd_up, odd_pairs, odd_pairs)
    from_even_up = swap(even_up, behind, [])
    wide = jax.ShapeDtypeStruct((funcs, ROWS, WINDOW), jnp.bfloat16)
    prepared = call(
        prepare_kernel,
        (
            wide,
            jax.ShapeDtypeStruct((ROWS, funcs * WINDOW), jnp.bfloat16),
            jax.ShapeDtypeStruct((WINDOW, WINDOW), jnp.bfloat16),
            jax.ShapeDtypeStruct((ROWS, WINDOW), jnp.bfloat16),
            message,
        ),
        [VMEM, VMEM, VMEM, SMEM, SMEM, VMEM],
        "window_layout",
        0,
        2 << 20,
    )(three_center, metric_tensor, spread, pattern, block_size, from_first_even)
    lead = funcs_at - 5
    order = [lead] + [i for i in range(funcs_at) if i != lead]
    partial_sum = call(
        functools.partial(main_kernel, [order.index(i) for i in range(funcs_at)]),
        jax.ShapeDtypeStruct((ROWS // 8, 8, WIDTH), jnp.bfloat16),
        [VMEM] * 7,
        "exchange_terms",
        1 << 28,
        2 << 20,
        [pltpu.VMEM((WINDOW, WINDOW), jnp.bfloat16)],
    )(*prepared, from_odd_up, from_even_up)
    terms = lax.all_to_all(partial_sum, "aux", 0, 0, axis_index_groups=[order])
    return jnp.sum(terms.astype(jnp.float32), axis=0).astype(jnp.bfloat16)


def solution(mesh):
    placed = (P("orb", "aux"), P("orb", "aux"), P("orb", None), P("orb", None), P())
    return jax.shard_map(
        on_device, mesh=mesh, in_specs=placed, out_specs=P(("orb", "aux"), None), check_vma=False
    )
```
